32 devices in a mesh: groups: 2 (over x), shard: 16 (over z, y, core).
Axes of the slice: x: 2, y: 2, z: 4, core: 2. Of those that a mesh axis runs over, the one named last changes fastest.
Arguments:
- query_grads: bfloat16 [256, 8, 4096], P(('groups', 'shard')), parts along dimension 0, may hold values from -6 to 6
- query_routes: int32 [256, 8], P('groups'), parts along dimension 0, may hold values from 0 to 31, all different within a row; in each aligned block of 8 rows (0 to 7, 8 to 15, ...) at most 4 rows name the same one
- train_grads: bfloat16 [4096, 8, 4096], P(('groups', 'shard')), parts along dimension 0, may hold values from -6 to 6
- train_routes: int32 [4096, 8], P(('groups', 'shard')), parts along dimension 0, may hold values from 0 to 31, all different within a row; in each aligned block of 128 rows (0 to 127, 128 to 255, ...) at most 64 rows name the same one
- train_counts: int32 [32], P(('groups', 'shard')), parts along dimension 0, may hold values from 1 to 128, 1536 in all
- owner_slot: int32 [32], replicated, may hold values from 0 to 31, each once
- basis_s: float32 [32, 64, 64], P('shard'), may hold values from -0.75 to 0.75
- basis_a: float32 [32, 64, 64], P('shard'), may hold values from -0.75 to 0.75
- eigenvalues: float32 [32, 64, 64], P('shard'), may hold values from 0.05 to 5
Outputs:
- scores: float32 [256, 2048], P('groups', 'shard'), parts along dimension 0
The draws below stay inside these ranges and needn't reach their ends.
There are 2 independent parts, one for each index of `groups`. The reference program is written for one: setup_inputs(seed, part) draws one part's arguments, and reference() takes and returns one part's arrays. A program takes and returns all parts, laid end to end along the dimension named above; an argument that names none is the same for every part. Nothing has to cross between parts.
Inputs may be any that keep to these rules, and one draw needn't show every extreme that they name: `query_routes`: in each aligned block of 8 query rows no expert is named by more than 4 rows. `train_routes`: in each aligned block of 128 train rows no expert is named by more than 64 rows.
All inputs are finite; a program needn't handle non-finite values. No bound on the sum of `train_counts` on one device may be relied on, other than what follows from the above.
Results may differ from the reference program's by a relative error of at most 0.0029.
Values may be sent and summed in bfloat16 or wider, within the bound.
No kernel may reach another device: no remote copies, remote signals or barrier semaphores. Data moves between devices by JAX's collectives and lax.ppermute only.
A program may use at most 128 MiB of HBM per device.

```python
import math
import jax
import jax.numpy as jnp
import numpy as np
from jax import lax

FAC = 64
GRAD = 4096
TOP = 8
E = 32
QDEV = 8
TR_DEV = 128
Q = 128
TRAIN = 2048
MQ = 4
CAPT = 64
N_SHARD = 16


def levels(stream_key, shape, cuts, smallest, top_value):
    gain = 1.0
    for position, blocks in cuts:
        draws = jax.random.uniform(jax.random.fold_in(jax.random.fold_in(stream_key, 6), position), (blocks,), jnp.float32, smallest / len(cuts), top_value / len(cuts))
        gain = gain * jnp.repeat(jnp.exp(draws), shape[position] // blocks).reshape((-1,) + (1,) * (len(shape) - 1 - position))
    return gain


def split_up(amount, total, most, lean):
    portions = [(1 << 20) // math.isqrt(standing ** lean) + 1 for standing in range(2, amount + 1)]
    surplus, counts = total - most - (amount - 1), [1] * (amount - 1)
    while surplus > 0:
        movable = [i for i in range(amount - 1) if counts[i] < most]
        pool, budget = sum([portions[i] for i in movable]), surplus
        for i in movable:
            extra = min(most - counts[i], max(1, budget * portions[i] // pool), surplus)
            counts[i] = counts[i] + extra
            surplus = surplus - extra
    return np.array([most] + counts)


def uneven(own_key, number_of, total, most, lean):
    if number_of == 2:
        one = jax.random.randint(own_key, (), max(1, total - most), min(most, total - 1) + 1)
        return jnp.stack([one, total - one])
    sizes = jnp.asarray(split_up(number_of, total, most, lean), jnp.int32)
    couples = (number_of - 1) // 2
    donor, receiver = sizes[1:1 + 2 * couples:2], sizes[2:2 + 2 * couples:2]
    slack = jnp.minimum(donor - 1, most - receiver)
    passed = jax.random.randint(jax.random.fold_in(own_key, 1), (couples,), 0, 1 << 20) % (slack + 1)
    sizes = sizes.at[1:1 + 2 * couples:2].set(donor - passed).at[2:2 + 2 * couples:2].set(receiver + passed)
    return sizes[jax.random.permutation(jax.random.fold_in(own_key, 2), number_of)]


def routed_block(own_key, own, number, rows, amount, top, bound, skew):
    ranking = jax.random.permutation(own_key, amount)
    heavy_load, usual = shares(amount, rows * top, bound, skew, True), shares(amount, rows * top, bound, skew, False)
    places = jnp.arange(amount)

    def named(sizes, turn):
        used = int((sizes > 0).sum())
        fixed = max(1, used // 4)
        passed = fixed + (places - fixed + turn * (used - fixed)) % max(1, amount - fixed)
        return jnp.zeros((amount,), jnp.int32).at[ranking[jnp.where(places < fixed, places, passed)]].set(jnp.asarray(sizes, jnp.int32))

    sizes = jnp.where(number % 4 == 0, named(heavy_load, number // 4), named(usual, number - number // 4 - 1))
    mixed = jax.random.permutation(jax.random.fold_in(own, 3), amount)
    giver, sink = mixed[0:amount // 2 * 2:2], mixed[1:amount // 2 * 2:2]
    slack = jnp.minimum(sizes[giver] - 1, bound - sizes[sink]) // 2
    slack = jnp.where((giver == ranking[0]) | (sink == ranking[0]) | (sizes[sink] == 0), 0, jnp.maximum(slack, 0))
    passed = jax.random.randint(jax.random.fold_in(own, 4), (amount // 2,), 0, 1 << 20) % (slack + 1)
    sizes = sizes.at[giver].add(-passed).at[sink].add(passed)
    items = jnp.searchsorted(jnp.cumsum(sizes), jnp.arange(rows * top), side="right").astype(jnp.int32)
    listing = items.reshape(top, rows).T
    listing = listing[jax.random.permutation(jax.random.fold_in(own, 1), rows)]
    turn = jax.random.randint(jax.random.fold_in(own, 2), (rows, 1), 0, top)
    return jnp.take_along_axis(listing, (jnp.arange(top)[None, :] + turn) % top, axis=1)


def shares(number_of, total, limit, skew, full):
    loads = [(1 << 20) // math.isqrt(grade ** skew) + 1 for grade in range(1, number_of + 1)]
    largest = limit if full else min(limit, max(-(-total // number_of), total * loads[0] // sum(loads)))
    least = 1 if total - largest >= number_of - 1 else 0
    given, spare = [largest] + [least] * (number_of - 1), total - largest - least * (number_of - 1)
    while spare > 0:
        free = [i for i in range(1, number_of) if given[i] < largest] or [i for i in range(1, number_of) if given[i] < limit]
        mass, left = sum([loads[i] for i in free]), spare
        for i in free:
            more = min(limit - given[i], max(1, left * loads[i] // mass), spare)
            given[i] = given[i] + more
            spare = spare - more
    return np.array(given)


def noise(stream_key, extent, spread, bound, cuts=(), held_as=jnp.bfloat16):
    result = jax.random.normal(stream_key, extent, jnp.float32) * spread
    if len(cuts) > 0:
        result = levels(stream_key, extent, cuts, -0.22, 0.18) * result
    return jnp.clip(result, min=-bound, max=bound).astype(held_as)


def setup_inputs(seed: int = 0, part: int = 0) -> dict:
    streams_of = jax.random.split(jax.random.key(seed), 10)
    part_splits = jax.random.split(jax.random.fold_in(streams_of[9], part), 10)
    query_grads = noise(part_splits[0], (Q, TOP, GRAD), 1.0, 6.0, ((0, 16),))
    query_routes_keys = jax.random.split(jax.random.fold_in(part_splits[1], 1), Q // QDEV)
    query_routes_turns = jax.random.permutation(jax.random.fold_in(part_splits[1], 3), Q // QDEV)
    query_routes = jax.vmap(lambda own, number: routed_block(jax.random.fold_in(part_splits[1], 2), own, number, QDEV, E, TOP, MQ, 2))(query_routes_keys, query_routes_turns).reshape((Q, TOP))
    train_grads = noise(part_splits[2], (TRAIN, TOP, GRAD), 1.0, 6.0, ((0, 16),))
    train_routes_keys = jax.random.split(jax.random.fold_in(part_splits[3], 1), TRAIN // TR_DEV)
    train_routes_turns = jax.random.permutation(jax.random.fold_in(part_splits[3], 3), TRAIN // TR_DEV)
    train_routes = jax.vmap(lambda own, number: routed_block(jax.random.fold_in(part_splits[3], 2), own, number, TR_DEV, E, TOP, CAPT, 2))(train_routes_keys, train_routes_turns).reshape((TRAIN, TOP))
    train_counts = uneven(part_splits[4], N_SHARD, TR_DEV * N_SHARD * 3 // 4, TR_DEV, 2).astype(jnp.int32)
    owner_slot = jax.random.permutation(streams_of[5], E).astype(jnp.int32)
    basis_s = noise(streams_of[6], (E, FAC, FAC), FAC ** -0.5, 0.75, ((0, 16),), jnp.float32)
    basis_a = noise(streams_of[7], (E, FAC, FAC), FAC ** -0.5, 0.75, ((0, 16),), jnp.float32)
    eigenvalues = jnp.clip(jnp.exp(math.log(5.0) - 4.6051702 * jax.random.uniform(streams_of[8], (E, FAC, FAC), jnp.float32) ** levels(streams_of[8], (E, FAC, FAC), ((0, 16),), -0.2, 0.2)), 0.05, 5.0)
    return {"query_grads": query_grads, "query_routes": query_routes, "train_grads": train_grads, "train_routes": train_routes, "train_counts": train_counts, "owner_slot": owner_slot, "basis_s": basis_s, "basis_a": basis_a, "eigenvalues": eigenvalues}


DAMPING = 0.01


def precondition(grads, basis_s, basis_a, eigenvalues):
    count = grads.shape[0]
    slots = grads.shape[1]
    order = basis_s.shape[-1]
    field = grads.reshape(count, slots, order, order).astype(jnp.float32)
    turned = jnp.einsum('eji,ecjk->ecik', basis_s, field, precision=lax.Precision.HIGHEST)
    turned = jnp.einsum('ecik,ekl->ecil', turned, basis_a, precision=lax.Precision.HIGHEST)
    scaled = turned / (eigenvalues[:, None] + DAMPING)
    back = jnp.einsum('eij,ecjk->ecik', basis_s, scaled, precision=lax.Precision.HIGHEST)
    back = jnp.einsum('ecik,elk->ecil', back, basis_a, precision=lax.Precision.HIGHEST)
    return back.reshape(count, slots, order * order).astype(jnp.bfloat16)


def reference(query_grads, query_routes, train_grads, train_routes, train_counts, owner_slot, basis_s, basis_a, eigenvalues):
    slot_rows = owner_slot[query_routes].reshape(-1)
    flat_grads = query_grads.reshape(Q * TOP, 1, GRAD)
    preconditioned = precondition(flat_grads, basis_s[slot_rows], basis_a[slot_rows], eigenvalues[slot_rows]).reshape(Q, TOP, GRAD)
    positions = jnp.arange(TRAIN, dtype=jnp.int32)
    live = (positions % TR_DEV) < train_counts[positions // TR_DEV]
    query_cap = N_SHARD * MQ
    train_cap = N_SHARD * CAPT

    def one_expert(total, expert):
        query_hit = query_routes == expert
        query_has = jnp.any(query_hit, axis=1)
        query_index = jnp.nonzero(query_has, size=query_cap, fill_value=0)[0].astype(jnp.int32)
        query_ok = jnp.arange(query_cap, dtype=jnp.int32) < jnp.sum(query_has.astype(jnp.int32))
        query_slot = jnp.argmax(query_hit[query_index].astype(jnp.int32), axis=1).astype(jnp.int32)
        query_block = preconditioned[query_index, query_slot]
        train_hit = train_routes == expert
        train_has = jnp.any(train_hit, axis=1) & live
        train_index = jnp.nonzero(train_has, size=train_cap, fill_value=0)[0].astype(jnp.int32)
        train_ok = jnp.arange(train_cap, dtype=jnp.int32) < jnp.sum(train_has.astype(jnp.int32))
        train_slot = jnp.argmax(train_hit[train_index].astype(jnp.int32), axis=1).astype(jnp.int32)
        train_block = train_grads[train_index, train_slot]
        products = jnp.dot(query_block, train_block.T, preferred_element_type=jnp.float32)
        products = jnp.where(query_ok[:, None] & train_ok[None, :], products, jnp.float32(0.0))
        total = total.at[query_index[:, None], train_index[None, :]].add(products)
        return total, None

    start = jnp.zeros((Q, TRAIN), jnp.float32)
    scores, unused = lax.scan(one_expert, start, jnp.arange(E, dtype=jnp.int32))
    return scores
```

```python
import functools

import jax
import jax.numpy as jnp
from jax import lax
from jax.experimental import pallas as pl
from jax.experimental.pallas import tpu as pltpu
from jax.sharding import PartitionSpec as P

DAMPING = 0.01
F32, BF16 = jnp.float32, jnp.bfloat16
RAW_HOPS = 0
STRIDE = 65
GROUP = 32
TILE = 256
MIB = 2**20


def split(x):
    hi = x.astype(BF16)
    return hi, (x - hi.astype(F32)).astype(BF16)


def swap(x):
    return pltpu.roll(x, 64, 1)


def precondition_kernel(chunks, experts, routes, owner, place, devs, mine, sib, *rest):
    raws, outs = rest[:chunks], rest[chunks : 2 * chunks]
    tab_a, tab_at, tab_s, tab_st, scale, xs, ys = rest[2 * chunks :]
    half = experts // 2
    left64 = lax.broadcasted_iota(jnp.int32, (64, 128), 1) < 64
    left = left64[:32]

    def prepare(e, src, at):
        base = pl.multiple_of(e * 96, 32)

        def twice(f):
            r = swap(f)
            return jnp.concatenate([jnp.where(left, f, r), jnp.where(left, r, f)], 0)

        s = twice(src[pl.ds(base, 32), :])
        a = twice(src[pl.ds(base + 32, 32), :])
        scale[at + e] = 1.0 / (twice(src[pl.ds(base + 64, 32), :]) + DAMPING)
        t = jnp.concatenate([s, a], 0).T[:64]
        r = swap(t)
        st, a_t = jnp.where(left64, t, r), jnp.where(left64, r, t)
        for ref, m in ((tab_s, s), (tab_st, st)):
            hi, lo = split(m)
            ref[at + e, :, :128] = hi
            ref[at + e, :, 128:] = lo
        for ref, m in ((tab_a, a), (tab_at, a_t)):
            for w in (0, 1):
                hi, lo = split(jnp.where(left64 if w == 0 else ~left64, m, 0.0))
                ref[at + e, w, :64] = hi
                ref[at + e, w, 64:] = lo

    def both(e, unused):
        prepare(e, mine, 0)
        prepare(e, sib, half)
        return 0

    lax.fori_loop(0, half, both, 0, unroll=2)

    def pair(tab, e1, e2, three):
        hi = [tab[e1, 0, :64], tab[e2, 1, :64]]
        lo = [tab[e1, 0, 64:], tab[e2, 1, 64:]]
        return jnp.concatenate(hi + (hi if three else []) + lo, 0)

    def cross(tab, e1, e2, x):
        hi, lo = split(x)
        o = jnp.dot(
            jnp.concatenate([tab[e1], tab[e2]], 0),
            jnp.concatenate([hi, lo, hi, lo], 0),
            preferred_element_type=F32,
        )
        return jnp.where(left64, o[:64], o[64:])

    for ch in range(chunks):
        raw, out = raws[ch], outs[ch]
        for c in range(32):
            xs[pl.ds(c * STRIDE, 64), :] = raw[:, c * 128 : (c + 1) * 128].astype(F32)

        def group(b, unused):
            es, g, x = [], [], []
            for i in range(GROUP):
                row = b * GROUP + i
                es.append(place[owner[routes[devs[ch] * 8 + row // 8, row % 8]]])
                g.append(xs[pl.ds(row, 32, stride=STRIDE), :])
            n = GROUP // 2
            ee = [(es[2 * p], es[2 * p + 1]) for p in range(n)]
            for p in range(n):
                g1, g2 = g[2 * p], g[2 * p + 1]
                h = [jnp.where(left, g1, swap(g2)), jnp.where(left, swap(g1), g2)]
                h = jnp.concatenate(h, 0).astype(BF16)
                h = jnp.concatenate([h, h], 1)
                x.append(jnp.dot(h, pair(tab_a, *ee[p], False), preferred_element_type=F32))
            x = [
                cross(tab_st, *ee[p], x[p]) * jnp.where(left64, scale[ee[p][0]], scale[ee[p][1]])
                for p in range(n)
            ]
            x = [cross(tab_s, *ee[p], x[p]) for p in range(n)]
            for p in range(n):
                hi, lo = split(x[p])
                h = jnp.concatenate([hi, lo, hi], 1)
                y = jnp.dot(h, pair(tab_at, *ee[p], True), preferred_element_type=F32)
                top, low = y[:32], y[32:]
                for w, v in enumerate((jnp.where(left, top, swap(low)), jnp.where(left, swap(top), low))):
                    row = b * GROUP + 2 * p + w
                    ys[pl.ds((row % 8) * 8 + row // 8, 32, stride=STRIDE), :] = v
            return 0

        lax.fori_loop(0, 64 // GROUP, group, 0)
        for c in range(32):
            out[:, c * 128 : (c + 1) * 128] = ys[pl.ds(c * STRIDE, 64), :].astype(BF16)


def precondition(routes, owner, place, devs, mine, sib, raws):
    experts = owner.shape[0]
    chunks = len(raws)
    sm = pl.BlockSpec(memory_space=pltpu.SMEM)
    vm = pl.BlockSpec(memory_space=pltpu.VMEM)
    return pl.pallas_call(
        functools.partial(precondition_kernel, chunks, experts),
        out_shape=[jax.ShapeDtypeStruct(r.shape, BF16) for r in raws],
        in_specs=[sm] * 4 + [vm] * (2 + chunks),
        out_specs=[vm] * chunks,
        scratch_shapes=[
            pltpu.VMEM((experts, 2, 128, 128), BF16),
            pltpu.VMEM((experts, 2, 128, 128), BF16),
            pltpu.VMEM((experts, 64, 256), BF16),
            pltpu.VMEM((experts, 64, 256), BF16),
            pltpu.VMEM((experts, 64, 128), F32),
            pltpu.VMEM((32 * STRIDE, 128), F32),
            pltpu.VMEM((32 * STRIDE, 128), F32),
        ],
        compiler_params=pltpu.CompilerParams(vmem_limit_bytes=32 * MIB),
        cost_estimate=pl.CostEstimate(
            flops=10**9 * (2 + 3 * chunks), bytes_accessed=10**6 * (1 + chunks), transcendentals=0
        ),
        name="precondition",
    )(routes, owner, place, devs, mine, sib, *raws)


def products_kernel(rows, earlier, tiles, devs, own_route, sib_route, query_route, own_train, sib_train, *rest):
    n_in = len(rows)
    parts, old = rest[:n_in], rest[n_in : n_in + 2 * len(earlier)]
    out_own, out_sib, held, total = rest[n_in + 2 * len(earlier) :]
    step = pl.program_id(0)
    units = sum(rows) // 64
    train_rows = tiles * TILE

    @pl.when(step == 0)
    def _():
        at = 0
        for part, r in zip(parts, rows):
            held[at : at + r, :] = part[...]
            at += r

    def one(train, route, base, i):
        g = lax.dot_general(held[...], train[...], (((1,), (1,)), ((), ())), preferred_element_type=F32)
        column = pl.multiple_of(i * TILE, TILE)
        there = route[:, pl.ds(column, TILE)]
        for u in range(units):
            want = query_route[pl.ds(pl.multiple_of(devs[u] * 64, 64), 64), :]
            want = jnp.concatenate([want] * (TILE // 128), 1)
            hit = jnp.where(want == there, g[u * 64 : (u + 1) * 64], 0.0)
            total[u * 8 : (u + 1) * 8, pl.ds(base + column, TILE)] = jnp.sum(hit.reshape(8, 8, TILE), axis=0)

    @pl.when(step < tiles)
    def _():
        one(own_train, own_route, 0, step)

    @pl.when(step >= tiles)
    def _():
        one(sib_train, sib_route, train_rows, step - tiles)

    @pl.when(step == 2 * tiles - 1)
    def _():
        row = lax.broadcasted_iota(jnp.int32, (train_rows, 128), 0)
        col = lax.broadcasted_iota(jnp.int32, (train_rows, 128), 1)
        fold = (lax.shift_right_logical(row, 3) == col).astype(BF16)

        def folded(x):
            hi = x.astype(BF16)
            left = x - hi.astype(F32)
            mid = left.astype(BF16)
            low = (left - mid.astype(F32)).astype(BF16)
            y = jnp.dot(jnp.concatenate([hi, mid, low], 0), fold, preferred_element_type=F32)
            n = x.shape[0]
            return y[:n] + y[n : 2 * n] + y[2 * n :]

        for k, out in enumerate((out_own, out_sib)):
            now = folded(total[:, k * train_rows : (k + 1) * train_rows])
            if not earlier:
                out[...] = now
                continue
            at = 0
            for j, n_units in enumerate(list(earlier) + [units]):
                for u in range(n_units):
                    dev = devs[units + at] if j < len(earlier) else devs[u]
                    block = (old[2 * j + k] if j < len(earlier) else now)[u * 8 : (u + 1) * 8]
                    out[pl.ds(pl.multiple_of((dev // 2) * 8, 8), 8), :] = block
                    at += 1


def products(devs, own_route, sib_route, query_route, own_train, sib_train, parts, old, chips):
    rows = [p.shape[0] for p in parts]
    units = sum(rows) // 64
    train_rows, width = own_train.shape
    tiles = train_rows // TILE
    earlier = [o[0].shape[0] // 8 for o in old]
    flat_old = [v for o in old for v in o]
    sm = pl.BlockSpec(memory_space=pltpu.SMEM)
    whole = lambda v: pl.BlockSpec(v.shape, lambda i: (0,) * len(v.shape))
    n_out = chips * 8 if old else units * 8
    return pl.pallas_call(
        functools.partial(products_kernel, rows, earlier, tiles),
        grid=(2 * tiles,),
        out_shape=[jax.ShapeDtypeStruct((n_out, 128), F32)] * 2,
        in_specs=[sm, whole(own_route), whole(sib_route), whole(query_route)]
        + [
            pl.BlockSpec((TILE, width), lambda i: (jnp.minimum(i, tiles - 1), 0)),
            pl.BlockSpec((TILE, width), lambda i: (jnp.maximum(i - tiles, 0), 0)),
        ]
        + [whole(v) for v in list(parts) + flat_old],
        out_specs=[pl.BlockSpec((n_out, 128), lambda i: (0, 0))] * 2,
        scratch_shapes=[pltpu.VMEM((sum(rows), width), BF16), pltpu.VMEM((units * 8, 2 * train_rows), F32)],
        compiler_params=pltpu.CompilerParams(vmem_limit_bytes=32 * MIB),
        cost_estimate=pl.CostEstimate(
            flops=4 * 128 * max(1, (units + 1) // 2) * train_rows * width,
            bytes_accessed=4 * train_rows * width,
            transcendentals=0,
        ),
        name="products",
    )(devs, own_route, sib_route, query_route, own_train, sib_train, *parts, *flat_old)


def local(
    query_grads,
    query_routes,
    train_grads,
    train_routes,
    train_counts,
    owner_slot,
    basis_s,
    basis_a,
    eigenvalues,
):
    devices = lax.axis_size("shard")
    me = lax.axis_index("shard")
    experts = owner_slot.shape[0]
    queries, top = query_routes.shape
    width = query_grads.shape[2]
    train_dev = train_grads.shape[0]
    slots = basis_s.shape[0]
    chips = devices // 2
    far = chips // 2
    ring = [2 * z for z in range(far)] + [2 * z + 1 for z in reversed(range(far))]
    spot = [ring.index(c) for c in range(chips)]

    def shift(step):
        return [
            (2 * c + k, 2 * ring[(i + step) % chips] + k) for i, c in enumerate(ring) for k in range(2)
        ]

    ahead, back = shift(1), shift(-1)
    across = [(d, d ^ 1) for d in range(devices)]
    send = lambda v, way: lax.ppermute(v, "shard", way)

    def circulate(own, up, down, first, until=None):
        out = []
        for _ in range(first, far - 1):
            up, down = send(up, ahead), send(down, back)
            out.append((up, down))
        cut = own.shape[0] // 2
        out.append((send(up[:cut], ahead), send(down[cut:], back)))
        return out

    halves = lambda m: jnp.concatenate([m[:, :32], m[:, 32:]], axis=-1)
    pack = jnp.stack([basis_s.reshape(slots, 32, 128), halves(basis_a), halves(eigenvalues)], axis=1)
    pack = pack.reshape(slots * 96, 128)
    steps = circulate(pack, pack, pack, 0)
    mine = jnp.concatenate([pack] + [v for step in steps for v in step], axis=0)
    sib = send(mine, across)

    spots = jnp.asarray(spot, jnp.int32)
    my_spot = jnp.sum(jnp.where(jnp.arange(chips) == me // 2, spots, 0))
    rel = (jnp.repeat(spots, 2 * slots) - my_spot + chips) % chips
    order = jnp.where(rel > far, 2 * (chips - rel) - 1, 2 * rel)
    order = jnp.where(rel == far, chips - 1, order)
    slot = jnp.arange(experts, dtype=jnp.int32)
    core = (slot // slots) % 2
    place = (jnp.where(core == me % 2, 0, chips) + order) * slots + slot % slots

    rings = jnp.asarray(ring, jnp.int32)

    def dev_at(distance):
        at = (my_spot + distance) % chips
        return 2 * jnp.sum(jnp.where(jnp.arange(chips) == at, rings, 0)) + me % 2

    devs_of = lambda ds: jnp.stack([dev_at(d) for d in ds]).astype(jnp.int32)

    live = jnp.arange(train_dev, dtype=jnp.int32) < train_counts[0]
    own_route = jnp.where(live[:, None], train_routes, -1).reshape(1, train_dev * top)
    sib_route = send(own_route, across)
    own_train = train_grads.reshape(train_dev * top, width)
    sib_train = send(own_train, across)
    query_route = query_routes.reshape(devices, 8, top).transpose(0, 2, 1).reshape(queries * top, 1)
    query_route = jnp.broadcast_to(query_route, (queries * top, 128))

    raw = query_grads.reshape(-1, width)
    pre = lambda raws, ds: precondition(query_routes, owner_slot, place, devs_of(ds), mine, sib, raws)
    if RAW_HOPS == 0:
        own = pre([raw], [0])[0]
        steps = circulate(own, own, own, 0)
    else:
        up, down = send(raw, ahead), send(raw, back)
        up, down = pre([up, down], [-1, 1])
        own = pre([raw], [0])[0]
        steps = [(up, down)] + circulate(own, up, down, 1)

    calls = [([own, *steps[0]], [0, -1, 1])]
    for s in range(1, far - 1, 2):
        two = range(s, min(s + 2, far - 1))
        calls.append(([v for t in two for v in steps[t]], [d for t in two for d in (-t - 1, t + 1)]))
    done, ds = [], []
    for parts, distances in calls:
        done.append(
            products(devs_of(distances), own_route, sib_route, query_route, own_train, sib_train, parts, [], chips)
        )
        ds += distances
    here, there = products(
        devs_of([far] + ds), own_route, sib_route, query_route, own_train, sib_train, steps[-1], done, chips
    )
    other = send(there, across)
    here, other = here.reshape(chips, 8, train_dev), other.reshape(chips, 8, train_dev)
    even = me % 2 == 0
    both = jnp.stack([jnp.where(even, here, other), jnp.where(even, other, here)], axis=1)
    return both.reshape(queries, train_dev)


def solution(mesh):
    placed = (
        P(("groups", "shard"), None, None),
        P("groups", None),
        P(("groups", "shard"), None, None),
        P(("groups", "shard"), None),
        P(("groups", "shard")),
        P(),
        P("shard", None, None),
        P("shard", None, None),
        P("shard", None, None),
    )
    return jax.shard_map(
        local, mesh=mesh, in_specs=placed, out_specs=P("groups", "shard"), check_vma=False
    )
```

```python
import functools

import jax
import jax.numpy as jnp
import numpy as np
from jax import lax
from jax.experimental import pallas as pl
from jax.experimental.pallas import tpu as pltpu
from jax.sharding import PartitionSpec as P

DAMPING = 0.01
F32, BF16 = jnp.float32, jnp.bfloat16
RAW_HOPS = 1
STRIDE = 65
GROUP = 32
TILE = 512
MIB = 2**20


def split(x):
    hi = x.astype(BF16)
    return hi, (x - hi.astype(F32)).astype(BF16)


def swap(x):
    return pltpu.roll(x, 64, 1)


def prepare_kernel(experts, mine, sib, tab_a, tab_at, tab_s, tab_st, scale):
    half = experts // 2
    left64 = lax.broadcasted_iota(jnp.int32, (64, 128), 1) < 64
    left = left64[:32]

    def prepare(e, src, at):
        base = pl.multiple_of(e * 96, 32)

        def twice(f):
            r = swap(f)
            return jnp.concatenate([jnp.where(left, f, r), jnp.where(left, r, f)], 0)

        s = twice(src[pl.ds(base, 32), :])
        a = twice(src[pl.ds(base + 32, 32), :])
        scale[at + e] = 1.0 / (twice(src[pl.ds(base + 64, 32), :]) + DAMPING)
        t = jnp.concatenate([s, a], 0).T[:64]
        r = swap(t)
        st, a_t = jnp.where(left64, t, r), jnp.where(left64, r, t)
        for ref, m in ((tab_s, s), (tab_st, st)):
            hi, lo = split(m)
            ref[at + e, :, :128] = hi
            ref[at + e, :, 128:] = lo
        for ref, m in ((tab_a, a), (tab_at, a_t)):
            for w in (0, 1):
                hi, lo = split(jnp.where(left64 if w == 0 else ~left64, m, 0.0))
                ref[at + e, w, :64] = hi
                ref[at + e, w, 64:] = lo

    def both(e, unused):
        prepare(e, mine, 0)
        prepare(e, sib, half)
        return 0

    lax.fori_loop(0, half, both, 0, unroll=2)


def prepare(mine, sib, experts):
    vm = pl.BlockSpec(memory_space=pltpu.VMEM)
    return pl.pallas_call(
        functools.partial(prepare_kernel, experts),
        out_shape=[
            jax.ShapeDtypeStruct((experts, 2, 128, 128), BF16),
            jax.ShapeDtypeStruct((experts, 2, 128, 128), BF16),
            jax.ShapeDtypeStruct((experts, 64, 256), BF16),
            jax.ShapeDtypeStruct((experts, 64, 256), BF16),
            jax.ShapeDtypeStruct((experts, 64, 128), F32),
        ],
        in_specs=[vm] * 2,
        out_specs=[vm] * 5,
        compiler_params=pltpu.CompilerParams(vmem_limit_bytes=32 * MIB),
        cost_estimate=pl.CostEstimate(flops=2 * 10**9, bytes_accessed=8 * MIB, transcendentals=0),
        name="prepare",
    )(mine, sib)


def precondition_kernel(units, routes, owner, info, tab_a, tab_at, tab_s, tab_st, scale, *rest):
    chunks = len(units)
    experts = owner.shape[0]
    raws, outs = rest[:chunks], rest[chunks : 2 * chunks]
    xs, ys = rest[2 * chunks :]
    left64 = lax.broadcasted_iota(jnp.int32, (64, 128), 1) < 64
    left = left64[:32]

    def pair(tab, e1, e2, three):
        hi = [tab[e1, 0, :64], tab[e2, 1, :64]]
        lo = [tab[e1, 0, 64:], tab[e2, 1, 64:]]
        return jnp.concatenate(hi + (hi if three else []) + lo, 0)

    def cross(tab, e1, e2, x):
        hi, lo = split(x)
        o = jnp.dot(
            jnp.concatenate([tab[e1], tab[e2]], 0),
            jnp.concatenate([hi, lo, hi, lo], 0),
            preferred_element_type=F32,
        )
        return jnp.where(left64, o[:64], o[64:])

    for ch in range(chunks):
        raw, out = raws[ch], outs[ch]
        first = info[experts + units[ch]] * 8
        for c in range(32):
            xs[pl.ds(c * STRIDE, 64), :] = raw[:, c * 128 : (c + 1) * 128].astype(F32)

        def group(b, unused):
            es, g, x = [], [], []
            for i in range(GROUP):
                row = b * GROUP + i
                es.append(info[owner[routes[first + row // 8, row % 8]]])
                g.append(xs[pl.ds(row, 32, stride=STRIDE), :])
            n = GROUP // 2
            ee = [(es[2 * p], es[2 * p + 1]) for p in range(n)]
            for p in range(n):
                g1, g2 = g[2 * p], g[2 * p + 1]
                h = [jnp.where(left, g1, swap(g2)), jnp.where(left, swap(g1), g2)]
                h = jnp.concatenate(h, 0).astype(BF16)
                h = jnp.concatenate([h, h], 1)
                x.append(jnp.dot(h, pair(tab_a, *ee[p], False), preferred_element_type=F32))
            x = [
                cross(tab_st, *ee[p], x[p]) * jnp.where(left64, scale[ee[p][0]], scale[ee[p][1]])
                for p in range(n)
            ]
            x = [cross(tab_s, *ee[p], x[p]) for p in range(n)]
            for p in range(n):
                hi, lo = split(x[p])
                h = jnp.concatenate([hi, lo, hi], 1)
                y = jnp.dot(h, pair(tab_at, *ee[p], True), preferred_element_type=F32)
                top, low = y[:32], y[32:]
                for w, v in enumerate((jnp.where(left, top, swap(low)), jnp.where(left, swap(top), low))):
                    row = b * GROUP + 2 * p + w
                    ys[pl.ds((row % 8) * 8 + row // 8, 32, stride=STRIDE), :] = v
            return 0

        lax.fori_loop(0, 64 // GROUP, group, 0)
        for c in range(32):
            out[:, c * 128 : (c + 1) * 128] = ys[pl.ds(c * STRIDE, 64), :].astype(BF16)


def precondition(routes, owner, info, tables, raws, units):
    chunks = len(raws)
    sm = pl.BlockSpec(memory_space=pltpu.SMEM)
    vm = pl.BlockSpec(memory_space=pltpu.VMEM)
    return pl.pallas_call(
        functools.partial(precondition_kernel, units),
        out_shape=[jax.ShapeDtypeStruct(r.shape, BF16) for r in raws],
        in_specs=[sm] * 3 + [vm] * (5 + chunks),
        out_specs=[vm] * chunks,
        scratch_shapes=[pltpu.VMEM((32 * STRIDE, 128), F32), pltpu.VMEM((32 * STRIDE, 128), F32)],
        compiler_params=pltpu.CompilerParams(vmem_limit_bytes=24 * MIB),
        cost_estimate=pl.CostEstimate(
            flops=10**9 * 3 * chunks, bytes_accessed=10**6 * (7 + chunks), transcendentals=0
        ),
        name="precondition",
    )(routes, owner, info, *tables, *raws)


def products_kernel(units, placed, shapes, experts, info, route, query_route, train, *rest):
    n_in = len(shapes)
    n_old = 0 if placed is None else len(placed)
    parts, old = rest[:n_in], rest[n_in : n_in + n_old]
    out, held, total = rest[n_in + n_old :]
    blocks = sum(shapes) // 64
    train_rows = train.shape[0]
    at = 0
    for part, r in zip(parts, shapes):
        held[at : at + r, :] = part[...]
        at += r

    def tile(i, unused):
        here = pl.ds(pl.multiple_of(i * TILE, TILE), TILE)
        g = lax.dot_general(held[...], train[here, :], (((1,), (1,)), ((), ())), preferred_element_type=F32)
        there = route[:, here]
        for u in range(blocks):
            first = pl.multiple_of(info[experts + units[u]] * 64, 64)
            want = jnp.concatenate([query_route[pl.ds(first, 64), :]] * (TILE // 128), 1)
            hit = jnp.where(want == there, g[u * 64 : (u + 1) * 64], 0.0)
            total[u * 8 : (u + 1) * 8, here] = jnp.sum(hit.reshape(8, 8, TILE), axis=0)
        return 0

    lax.fori_loop(0, train_rows // TILE, tile, 0)
    row = lax.broadcasted_iota(jnp.int32, (train_rows, 128), 0)
    col = lax.broadcasted_iota(jnp.int32, (train_rows, 128), 1)
    fold = (lax.shift_right_logical(row, 3) == col).astype(BF16)
    x = total[...]
    hi = x.astype(BF16)
    left = x - hi.astype(F32)
    mid = left.astype(BF16)
    low = (left - mid.astype(F32)).astype(BF16)
    y = jnp.dot(jnp.concatenate([hi, mid, low], 0), fold, preferred_element_type=F32)
    n = blocks * 8
    y = y[:n] + y[n : 2 * n] + y[2 * n :]
    if placed is None:
        out[...] = y
        return
    todo = [(y, units)] + list(zip(old, placed))
    for values, names in todo:
        for u, name in enumerate(names):
            first = pl.multiple_of(info[experts + name] * 8, 8)
            out[pl.ds(first, 8), :] = values[u * 8 : (u + 1) * 8]


def products(info, experts, route, query_route, train, parts, units, old=None, placed=None, queries=0):
    shapes = [p.shape[0] for p in parts]
    blocks = sum(shapes) // 64
    train_rows, width = train.shape
    sm = pl.BlockSpec(memory_space=pltpu.SMEM)
    vm = pl.BlockSpec(memory_space=pltpu.VMEM)
    old = list(old or [])
    return pl.pallas_call(
        functools.partial(products_kernel, units, placed, shapes, experts),
        out_shape=jax.ShapeDtypeStruct((queries if placed else blocks * 8, 128), F32),
        in_specs=[sm] + [vm] * (3 + len(parts) + len(old)),
        out_specs=vm,
        scratch_shapes=[pltpu.VMEM((sum(shapes), width), BF16), pltpu.VMEM((blocks * 8, train_rows), F32)],
        compiler_params=pltpu.CompilerParams(vmem_limit_bytes=24 * MIB),
        cost_estimate=pl.CostEstimate(
            flops=4 * 128 * max(2, blocks) * train_rows * width // 2,
            bytes_accessed=2 * train_rows * width,
            transcendentals=0,
        ),
        name="products",
    )(info, route, query_route, train, *parts, *old)


def tables_of(devices, slots):
    chips = devices // 2
    far = chips // 2
    ring = [2 * z for z in range(far)] + [2 * z + 1 for z in reversed(range(far))]
    spot = [ring.index(c) for c in range(chips)]
    rows = []
    for me in range(devices):
        place = []
        for slot in range(devices * slots):
            rel = (spot[slot // slots // 2] - spot[me // 2]) % chips
            order = chips - 1 if rel == far else 2 * (chips - rel) - 1 if rel > far else 2 * rel
            across = (slot // slots) % 2 != me % 2
            place.append((across * chips + order) * slots + slot % slots)
        near = [2 * ring[(spot[me // 2] + d) % chips] + me % 2 for d in range(chips)]
        rows.append(place + near + [d ^ 1 for d in near])
    return ring, np.array(rows, np.int32)


def tie(value, other):
    return lax.optimization_barrier((value, other))[0]


def local(
    query_grads,
    query_routes,
    train_grads,
    train_routes,
    train_counts,
    owner_slot,
    basis_s,
    basis_a,
    eigenvalues,
):
    devices = lax.axis_size("shard")
    me = lax.axis_index("shard")
    experts = owner_slot.shape[0]
    queries, top = query_routes.shape
    width = query_grads.shape[2]
    train_dev = train_grads.shape[0]
    slots = basis_s.shape[0]
    chips = devices // 2
    far = chips // 2
    ring, constants = tables_of(devices, slots)
    info = lax.dynamic_index_in_dim(jnp.asarray(constants), me, 0, keepdims=False)

    def shift(step):
        return [
            (2 * c + k, 2 * ring[(i + step) % chips] + k) for i, c in enumerate(ring) for k in range(2)
        ]

    ahead, back = shift(1), shift(-1)
    across = [(d, d ^ 1) for d in range(devices)]
    send = lambda v, way: lax.ppermute(v, "shard", way)
    near = lambda distance: distance % chips
    other = lambda distance: chips + distance % chips

    raw = query_grads.reshape(-1, width)

    halves = lambda m: jnp.concatenate([m[:, :32], m[:, 32:]], axis=-1)
    pack = jnp.stack([basis_s.reshape(slots, 32, 128), halves(basis_a), halves(eigenvalues)], axis=1)
    pack = pack.reshape(slots * 96, 128)
    got, up, down = [pack], pack, pack
    for _ in range(far - 1):
        up, down = send(up, ahead), send(down, back)
        got += [up, down]
    cut = pack.shape[0] // 2
    got += [send(up[:cut], ahead), send(down[cut:], back)]
    mine = jnp.concatenate(got, axis=0)
    tables = prepare(mine, send(mine, across), experts)

    live = jnp.arange(train_dev, dtype=jnp.int32) < train_counts[0]
    route = jnp.where(live[:, None], train_routes, -1).reshape(1, train_dev * top)
    train = train_grads.reshape(train_dev * top, width)
    query_route = query_routes.reshape(devices, 8, top).transpose(0, 2, 1).reshape(queries * top, 1)
    query_route = jnp.broadcast_to(query_route, (queries * top, 128))

    pre = lambda raws, names: precondition(query_routes, owner_slot, info, tables, raws, names)
    multiply = lambda parts, names, **more: products(
        info, experts, route, query_route, train, parts, names, **more
    )
    if RAW_HOPS:
        up, down = send(raw, ahead), send(raw, back)
        up, down = pre([up, down], [near(-1), near(1)])
        held, names = [up, down], [near(-1), near(1)]
    else:
        (own,) = pre([raw], [near(0)])
        up, down = own, own
        held, names = [own], [near(0)]
    done, placed = [], []
    for step in range(1 + RAW_HOPS, far + 1):
        if done:
            up, down = tie((up, down), done[-1])
        if step == far:
            up, down = send(up[:32], ahead), send(down[32:], back)
        else:
            up, down = send(up, ahead), send(down, back)
        if RAW_HOPS and step == 2:
            (own,) = pre([raw], [near(0)])
            held, names = held + [own], names + [near(0)]
        parts = held + [send(v, across) for v in held]
        names = names + [n + chips for n in names]
        done.append(multiply(parts, names))
        placed.append(names)
        held, names = [up, down], [near(-step), near(step)]
    last = jnp.concatenate([up, down], axis=0)
    return multiply(
        [last, send(last, across)], [near(far), other(far)], old=done, placed=placed, queries=queries
    )


def solution(mesh):
    placed = (
        P(("groups", "shard"), None, None),
        P("groups", None),
        P(("groups", "shard"), None, None),
        P(("groups", "shard"), None),
        P(("groups", "shard")),
        P(),
        P("shard", None, None),
        P("shard", None, None),
        P("shard", None, None),
    )
    return jax.shard_map(
        local, mesh=mesh, in_specs=placed, out_specs=P("groups", "shard"), check_vma=False
    )
```

```python
import functools

import jax
import jax.numpy as jnp
import numpy as np
from jax import lax
from jax.experimental import pallas as pl
from jax.experimental.pallas import tpu as pltpu
from jax.sharding import PartitionSpec as P

DAMPING = 0.01
F32, BF16 = jnp.float32, jnp.bfloat16
RAW_HOPS = 2
STRIDE = 65
GROUP = 32
TILE = 512
MIB = 2**20


def split(x):
    hi = x.astype(BF16)
    return hi, (x - hi.astype(F32)).astype(BF16)


def swap(x):
    return pltpu.roll(x, 64, 1)


def prepare_kernel(experts, mine, sib, tab_a, tab_at, tab_s, tab_st, scale):
    half = experts // 2
    left64 = lax.broadcasted_iota(jnp.int32, (64, 128), 1) < 64

    def prepare(e, src, at):
        base = pl.multiple_of(e * 96, 96)
        f_s = jnp.concatenate([src[pl.ds(base + h, 32, stride=2), :] for h in (0, 1)], 0)
        f_a = src[pl.ds(base + 64, 64), :]
        f_l = src[pl.ds(base + 128, 64), :]

        def twice(f):
            r = swap(f)
            return jnp.where(left64, f, r), jnp.where(left64, r, f)

        for w0, (s, a, lam) in enumerate(zip(twice(f_s), twice(f_a), twice(f_l))):
            to = at + e + w0
            scale[to] = 1.0 / (lam + DAMPING)
            t = jnp.concatenate([s, a], 0).T[:64]
            r = swap(t)
            st, a_t = jnp.where(left64, t, r), jnp.where(left64, r, t)
            for ref, m in ((tab_s, s), (tab_st, st)):
                hi, lo = split(m)
                ref[to, :, :128] = hi
                ref[to, :, 128:] = lo
            for ref, m in ((tab_a, a), (tab_at, a_t)):
                for w in (0, 1):
                    hi, lo = split(jnp.where(left64 if w == 0 else ~left64, m, 0.0))
                    ref[to, w, :64] = hi
                    ref[to, w, 64:] = lo

    def both(e, unused):
        prepare(2 * e, mine, 0)
        prepare(2 * e, sib, half)
        return 0

    lax.fori_loop(0, half // 2, both, 0)


def prepare(mine, sib, experts):
    vm = pl.BlockSpec(memory_space=pltpu.VMEM)
    return pl.pallas_call(
        functools.partial(prepare_kernel, experts),
        out_shape=[
            jax.ShapeDtypeStruct((experts, 2, 128, 128), BF16),
            jax.ShapeDtypeStruct((experts, 2, 128, 128), BF16),
            jax.ShapeDtypeStruct((experts, 64, 256), BF16),
            jax.ShapeDtypeStruct((experts, 64, 256), BF16),
            jax.ShapeDtypeStruct((experts, 64, 128), F32),
        ],
        in_specs=[vm] * 2,
        out_specs=[vm] * 5,
        compiler_params=pltpu.CompilerParams(vmem_limit_bytes=4 * MIB),
        cost_estimate=pl.CostEstimate(flops=2 * 10**9, bytes_accessed=8 * MIB, transcendentals=0),
        name="prepare",
    )(mine, sib)


def precondition_kernel(units, routes, owner, info, tab_a, tab_at, tab_s, tab_st, scale, *rest):
    chunks = len(units)
    experts = owner.shape[0]
    raws, outs = rest[:chunks], rest[chunks : 2 * chunks]
    xs, ys = rest[2 * chunks :]
    left64 = lax.broadcasted_iota(jnp.int32, (64, 128), 1) < 64
    left = left64[:32]

    def pair(tab, e1, e2, three):
        hi = [tab[e1, 0, :64], tab[e2, 1, :64]]
        lo = [tab[e1, 0, 64:], tab[e2, 1, 64:]]
        return jnp.concatenate(hi + (hi if three else []) + lo, 0)

    def cross(tab, e1, e2, x):
        hi, lo = split(x)
        o = jnp.dot(
            jnp.concatenate([tab[e1], tab[e2]], 0),
            jnp.concatenate([hi, lo, hi, lo], 0),
            preferred_element_type=F32,
        )
        return jnp.where(left64, o[:64], o[64:])

    for ch in range(chunks):
        raw, out = raws[ch], outs[ch]
        first = info[experts + units[ch]] * 8
        for c in range(32):
            xs[pl.ds(c * STRIDE, 64), :] = raw[:, c * 128 : (c + 1) * 128].astype(F32)

        def group(b, unused):
            es, g, x = [], [], []
            for i in range(GROUP):
                row = b * GROUP + i
                es.append(info[owner[routes[first + row // 8, row % 8]]])
                g.append(xs[pl.ds(row, 32, stride=STRIDE), :])
            n = GROUP // 2
            ee = [(es[2 * p], es[2 * p + 1]) for p in range(n)]
            for p in range(n):
                g1, g2 = g[2 * p], g[2 * p + 1]
                h = [jnp.where(left, g1, swap(g2)), jnp.where(left, swap(g1), g2)]
                h = jnp.concatenate(h, 0).astype(BF16)
                h = jnp.concatenate([h, h], 1)
                x.append(jnp.dot(h, pair(tab_a, *ee[p], False), preferred_element_type=F32))
            x = [
                cross(tab_st, *ee[p], x[p]) * jnp.where(left64, scale[ee[p][0]], scale[ee[p][1]])
                for p in range(n)
            ]
            x = [cross(tab_s, *ee[p], x[p]) for p in range(n)]
            for p in range(n):
                hi, lo = split(x[p])
                h = jnp.concatenate([hi, lo, hi], 1)
                y = jnp.dot(h, pair(tab_at, *ee[p], True), preferred_element_type=F32)
                top, low = y[:32], y[32:]
                for w, v in enumerate((jnp.where(left, top, swap(low)), jnp.where(left, swap(top), low))):
                    row = b * GROUP + 2 * p + w
                    ys[pl.ds((row % 8) * 8 + row // 8, 32, stride=STRIDE), :] = v
            return 0

        lax.fori_loop(0, 64 // GROUP, group, 0)
        for c in range(32):
            out[:, c * 128 : (c + 1) * 128] = ys[pl.ds(c * STRIDE, 64), :].astype(BF16)


def precondition(routes, owner, info, tables, raws, units):
    chunks = len(raws)
    sm = pl.BlockSpec(memory_space=pltpu.SMEM)
    vm = pl.BlockSpec(memory_space=pltpu.VMEM)
    return pl.pallas_call(
        functools.partial(precondition_kernel, units),
        out_shape=[jax.ShapeDtypeStruct(r.shape, BF16) for r in raws],
        in_specs=[sm] * 3 + [vm] * (5 + chunks),
        out_specs=[vm] * chunks,
        scratch_shapes=[pltpu.VMEM((32 * STRIDE, 128), F32), pltpu.VMEM((32 * STRIDE, 128), F32)],
        compiler_params=pltpu.CompilerParams(vmem_limit_bytes=8 * MIB),
        cost_estimate=pl.CostEstimate(
            flops=10**9 * 3 * chunks, bytes_accessed=10**6 * (7 + chunks), transcendentals=0
        ),
        name="precondition",
    )(routes, owner, info, *tables, *raws)


def products_kernel(units, placed, shapes, experts, info, route, query_route, train, *rest):
    n_in = len(shapes)
    n_old = 0 if placed is None else len(placed)
    parts, old = rest[:n_in], rest[n_in : n_in + n_old]
    out, held, total = rest[n_in + n_old :]
    blocks = sum(shapes) // 64
    train_rows = train.shape[0]
    at = 0
    for part, r in zip(parts, shapes):
        held[at : at + r, :] = part[...]
        at += r

    def tile(i, unused):
        here = pl.ds(pl.multiple_of(i * TILE, TILE), TILE)
        g = lax.dot_general(held[...], train[here, :], (((1,), (1,)), ((), ())), preferred_element_type=F32)
        there = route[:, here]
        for u in range(blocks):
            first = pl.multiple_of(info[experts + units[u]] * 64, 64)
            want = jnp.concatenate([query_route[pl.ds(first, 64), :]] * (TILE // 128), 1)
            hit = jnp.where(want == there, g[u * 64 : (u + 1) * 64], 0.0)
            total[u * 8 : (u + 1) * 8, here] = jnp.sum(hit.reshape(8, 8, TILE), axis=0)
        return 0

    lax.fori_loop(0, train_rows // TILE, tile, 0)
    row = lax.broadcasted_iota(jnp.int32, (train_rows, 128), 0)
    col = lax.broadcasted_iota(jnp.int32, (train_rows, 128), 1)
    fold = (lax.shift_right_logical(row, 3) == col).astype(BF16)
    x = total[...]
    hi = x.astype(BF16)
    left = x - hi.astype(F32)
    mid = left.astype(BF16)
    low = (left - mid.astype(F32)).astype(BF16)
    y = jnp.dot(jnp.concatenate([hi, mid, low], 0), fold, preferred_element_type=F32)
    n = blocks * 8
    y = y[:n] + y[n : 2 * n] + y[2 * n :]
    if placed is None:
        out[...] = y
        return
    todo = [(y, units)] + list(zip(old, placed))
    for values, names in todo:
        for u, name in enumerate(names):
            first = pl.multiple_of(info[experts + name] * 8, 8)
            out[pl.ds(first, 8), :] = values[u * 8 : (u + 1) * 8]


def products(info, experts, route, query_route, train, parts, units, old=None, placed=None, queries=0):
    shapes = [p.shape[0] for p in parts]
    blocks = sum(shapes) // 64
    train_rows, width = train.shape
    sm = pl.BlockSpec(memory_space=pltpu.SMEM)
    vm = pl.BlockSpec(memory_space=pltpu.VMEM)
    old = list(old or [])
    return pl.pallas_call(
        functools.partial(products_kernel, units, placed, shapes, experts),
        out_shape=jax.ShapeDtypeStruct((queries if placed else blocks * 8, 128), F32),
        in_specs=[sm] + [vm] * (3 + len(parts) + len(old)),
        out_specs=vm,
        scratch_shapes=[pltpu.VMEM((sum(shapes), width), BF16), pltpu.VMEM((blocks * 8, train_rows), F32)],
        compiler_params=pltpu.CompilerParams(vmem_limit_bytes=14 * MIB),
        cost_estimate=pl.CostEstimate(
            flops=4 * 128 * max(2, blocks) * train_rows * width // 2,
            bytes_accessed=2 * train_rows * width,
            transcendentals=0,
        ),
        name="products",
    )(info, route, query_route, train, *parts, *old)


def tables_of(devices, slots):
    chips = devices // 2
    far = chips // 2
    ring = [2 * z for z in range(far)] + [2 * z + 1 for z in reversed(range(far))]
    spot = [ring.index(c) for c in range(chips)]
    rows = []
    for me in range(devices):
        place = []
        for slot in range(devices * slots):
            rel = (spot[slot // slots // 2] - spot[me // 2]) % chips
            order = chips - 1 if rel == far else 2 * (chips - rel) - 1 if rel > far else 2 * rel
            across = (slot // slots) % 2 != me % 2
            place.append((across * chips + order) * slots + slot % slots)
        near = [2 * ring[(spot[me // 2] + d) % chips] + me % 2 for d in range(chips)]
        rows.append(place + near + [d ^ 1 for d in near])
    return ring, np.array(rows, np.int32)


def tie(value, other):
    return lax.optimization_barrier((value, other))[0]


def local(
    query_grads,
    query_routes,
    train_grads,
    train_routes,
    train_counts,
    owner_slot,
    basis_s,
    basis_a,
    eigenvalues,
):
    devices = lax.axis_size("shard")
    me = lax.axis_index("shard")
    experts = owner_slot.shape[0]
    queries, top = query_routes.shape
    width = query_grads.shape[2]
    train_dev = train_grads.shape[0]
    slots = basis_s.shape[0]
    chips = devices // 2
    far = chips // 2
    ring, constants = tables_of(devices, slots)
    info = lax.dynamic_index_in_dim(jnp.asarray(constants), me, 0, keepdims=False)

    def shift(step):
        return [
            (2 * c + k, 2 * ring[(i + step) % chips] + k) for i, c in enumerate(ring) for k in range(2)
        ]

    ahead, back = shift(1), shift(-1)
    across = [(d, d ^ 1) for d in range(devices)]
    send = lambda v, way: lax.ppermute(v, "shard", way)
    near = lambda distance: distance % chips
    other = lambda distance: chips + distance % chips

    raw = query_grads.reshape(-1, width)

    raws = []
    for _ in range(RAW_HOPS):
        u, d = raws[-1] if raws else (raw, raw)
        raws.append((send(u, ahead), send(d, back)))
    pairs = lambda m: jnp.concatenate([m[0::2], m[1::2]], axis=-1)
    pack = jnp.stack([pairs(basis_s), pairs(basis_a), pairs(eigenvalues)], axis=1).reshape(slots * 96, 128)
    got, up, down = [pack], pack, pack
    for _ in range(far - 1):
        up, down = send(up, ahead), send(down, back)
        got += [up, down]
    if raws:
        up, down = tie((up, down), raws[0])
    cut = pack.shape[0] // 2
    got += [send(up[:cut], ahead), send(down[cut:], back)]
    mine = jnp.concatenate(got, axis=0)
    sib = send(mine, across)
    if len(raws) > 1:
        sib = tie(sib, raws[-1])
    tables = prepare(mine, sib, experts)

    live = jnp.arange(train_dev, dtype=jnp.int32) < train_counts[0]
    route = jnp.where(live[:, None], train_routes, -1).reshape(1, train_dev * top)
    train = train_grads.reshape(train_dev * top, width)
    query_route = query_routes.reshape(devices, 8, top).transpose(0, 2, 1).reshape(queries * top, 1)
    query_route = jnp.broadcast_to(query_route, (queries * top, 128))

    pre = lambda raws, names: precondition(query_routes, owner_slot, info, tables, raws, names)
    multiply = lambda parts, names, **more: products(
        info, experts, route, query_route, train, parts, names, **more
    )
    held, names, parts = [], [], [raw]
    if RAW_HOPS:
        up, down = pre(list(raws[-1]), [near(-RAW_HOPS), near(RAW_HOPS)])
        held, names = [up, down], [near(-RAW_HOPS), near(RAW_HOPS)]
        parts = [raw] + [v for pair in raws[:-1] for v in pair]
        parts = list(tie(tuple(parts), up))
    kinds = [near(0)] + [near(d) for h in range(1, RAW_HOPS) for d in (-h, h)]
    rest = pre(parts, kinds)
    if not RAW_HOPS:
        up, down = rest[0], rest[0]
    held, names = held + list(rest), names + kinds
    done, placed = [], []
    for step in range(1 + RAW_HOPS, far + 1):
        if done:
            up, down = tie((up, down), done[-1])
        if step == far:
            up, down = send(up[:32], ahead), send(down[32:], back)
        else:
            up, down = send(up, ahead), send(down, back)
        parts = held + [send(v, across) for v in held]
        names = names + [n + chips for n in names]
        done.append(multiply(parts, names))
        placed.append(names)
        held, names = [up, down], [near(-step), near(step)]
    last = jnp.concatenate([up, down], axis=0)
    return multiply(
        [last, send(last, across)], [near(far), other(far)], old=done, placed=placed, queries=queries
    )


def solution(mesh):
    placed = (
        P(("groups", "shard"), None, None),
        P("groups", None),
        P(("groups", "shard"), None, None),
        P(("groups", "shard"), None),
        P(("groups", "shard")),
        P(),
        P("shard", None, None),
        P("shard", None, None),
        P("shard", None, None),
    )
    return jax.shard_map(
        local, mesh=mesh, in_specs=placed, out_specs=P("groups", "shard"), check_vma=False
    )
```

```python
import functools

import jax
import jax.numpy as jnp
import numpy as np
from jax import lax
from jax.experimental import pallas as pl
from jax.experimental.pallas import tpu as pltpu
from jax.sharding import PartitionSpec as P

DAMPING = 0.01
F32, BF16 = jnp.float32, jnp.bfloat16
STRIDE = 65
GROUP = 64
TILE = 512
MIB = 2**20


def split(x):
    hi = x.astype(BF16)
    return hi, (x - hi.astype(F32)).astype(BF16)


def swap(x):
    return pltpu.roll(x, 64, 1)


def prepare_kernel(at, count, src, *rest):
    tab_a, tab_at, tab_s, tab_st, scale = rest[-5:]
    left64 = lax.broadcasted_iota(jnp.int32, (64, 128), 1) < 64

    def both(pair, unused):
        e = 2 * pair
        base = pl.multiple_of(pair * 192, 192)
        f_s = jnp.concatenate([src[pl.ds(base + h, 32, stride=2), :] for h in (0, 1)], 0)
        f_a = src[pl.ds(base + 64, 64), :]
        f_l = src[pl.ds(base + 128, 64), :]

        def twice(f):
            r = swap(f)
            return jnp.where(left64, f, r), jnp.where(left64, r, f)

        for w0, (s, a, lam) in enumerate(zip(twice(f_s), twice(f_a), twice(f_l))):
            to = at + e + w0
            scale[to] = 1.0 / (lam + DAMPING)
            t = jnp.concatenate([s, a], 0).T[:64]
            r = swap(t)
            st, a_t = jnp.where(left64, t, r), jnp.where(left64, r, t)
            for ref, m in ((tab_s, s), (tab_st, st)):
                hi, lo = split(m)
                ref[to, :, :128] = hi
                ref[to, :, 128:] = lo
            for ref, m in ((tab_a, a), (tab_at, a_t)):
                for w in (0, 1):
                    hi, lo = split(jnp.where(left64 if w == 0 else ~left64, m, 0.0))
                    ref[to, w, :64] = hi
                    ref[to, w, 64:] = lo
        return 0

    lax.fori_loop(0, count // 2, both, 0, unroll=2)


def prepare(src, experts, at, tables=()):
    vm = pl.BlockSpec(memory_space=pltpu.VMEM)
    return pl.pallas_call(
        functools.partial(prepare_kernel, at, experts // 2),
        out_shape=[
            jax.ShapeDtypeStruct((experts, 2, 128, 128), BF16),
            jax.ShapeDtypeStruct((experts, 2, 128, 128), BF16),
            jax.ShapeDtypeStruct((experts, 64, 256), BF16),
            jax.ShapeDtypeStruct((experts, 64, 256), BF16),
            jax.ShapeDtypeStruct((experts, 64, 128), F32),
        ],
        in_specs=[vm] * (1 + len(tables)),
        out_specs=[vm] * 5,
        input_output_aliases={1 + i: i for i in range(len(tables))},
        compiler_params=pltpu.CompilerParams(vmem_limit_bytes=4 * MIB),
        cost_estimate=pl.CostEstimate(flops=10**9, bytes_accessed=4 * MIB, transcendentals=0),
        name="prepare",
    )(src, *tables)


def pack_kernel(s, a, lam, out):
    for i, m in enumerate((s, a, lam)):
        for p in range(m.shape[0] // 2):
            first = (3 * p + i) * 64
            out[first : first + 64, :] = jnp.concatenate([m[2 * p], m[2 * p + 1]], axis=1)


def pack_factors(s, a, lam):
    vm = pl.BlockSpec(memory_space=pltpu.VMEM)
    return pl.pallas_call(
        pack_kernel,
        out_shape=jax.ShapeDtypeStruct((s.shape[0] * 96, 128), F32),
        in_specs=[vm] * 3,
        out_specs=vm,
        compiler_params=pltpu.CompilerParams(vmem_limit_bytes=4 * MIB),
        cost_estimate=pl.CostEstimate(flops=10**5, bytes_accessed=10**5, transcendentals=0),
        name="pack",
    )(s, a, lam)


def precondition_kernel(units, routes, owner, info, tab_a, tab_at, tab_s, tab_st, scale, *rest):
    chunks = len(units)
    experts = owner.shape[0]
    raws, outs = rest[:chunks], rest[chunks : 2 * chunks]
    xs, ys = rest[2 * chunks :]
    left64 = lax.broadcasted_iota(jnp.int32, (64, 128), 1) < 64
    left = left64[:32]

    def pair(tab, e1, e2, three):
        hi = [tab[e1, 0, :64], tab[e2, 1, :64]]
        lo = [tab[e1, 0, 64:], tab[e2, 1, 64:]]
        return jnp.concatenate(hi + (hi if three else []) + lo, 0)

    def cross(tab, e1, e2, x):
        hi, lo = split(x)
        o = jnp.dot(
            jnp.concatenate([tab[e1], tab[e2]], 0),
            jnp.concatenate([hi, lo, hi, lo], 0),
            preferred_element_type=F32,
        )
        return jnp.where(left64, o[:64], o[64:])

    for ch in range(chunks):
        raw, out = raws[ch], outs[ch]
        first = info[experts + units[ch]] * 8
        for c in range(32):
            xs[pl.ds(c * STRIDE, 64), :] = raw[:, c * 128 : (c + 1) * 128].astype(F32)

        def group(b, unused):
            es, g, x = [], [], []
            for i in range(GROUP):
                row = b * GROUP + i
                es.append(info[owner[routes[first + row % 8, row // 8]]])
                g.append(xs[pl.ds(row, 32, stride=STRIDE), :])
            n = GROUP // 2
            ee = [(es[2 * p], es[2 * p + 1]) for p in range(n)]
            for p in range(n):
                g1, g2 = g[2 * p], g[2 * p + 1]
                h = [jnp.where(left, g1, swap(g2)), jnp.where(left, swap(g1), g2)]
                h = jnp.concatenate(h, 0).astype(BF16)
                h = jnp.concatenate([h, h], 1)
                x.append(jnp.dot(h, pair(tab_a, *ee[p], False), preferred_element_type=F32))
            x = [
                cross(tab_st, *ee[p], x[p]) * jnp.where(left64, scale[ee[p][0]], scale[ee[p][1]])
                for p in range(n)
            ]
            x = [cross(tab_s, *ee[p], x[p]) for p in range(n)]
            for p in range(n):
                hi, lo = split(x[p])
                h = jnp.concatenate([hi, lo, hi], 1)
                y = jnp.dot(h, pair(tab_at, *ee[p], True), preferred_element_type=F32)
                top, low = y[:32], y[32:]
                for w, v in enumerate((jnp.where(left, top, swap(low)), jnp.where(left, swap(top), low))):
                    row = b * GROUP + 2 * p + w
                    ys[pl.ds(row, 32, stride=STRIDE), :] = v
            return 0

        lax.fori_loop(0, 64 // GROUP, group, 0)
        for c in range(32):
            out[:, c * 128 : (c + 1) * 128] = ys[pl.ds(c * STRIDE, 64), :].astype(BF16)


def precondition(routes, owner, info, tables, raws, units):
    chunks = len(units)
    sm = pl.BlockSpec(memory_space=pltpu.SMEM)
    vm = pl.BlockSpec(memory_space=pltpu.VMEM)
    return pl.pallas_call(
        functools.partial(precondition_kernel, units),
        out_shape=[jax.ShapeDtypeStruct((64, raws[0].shape[1]), BF16)] * chunks,
        in_specs=[sm] * 3 + [vm] * (5 + len(raws)),
        out_specs=[vm] * chunks,
        scratch_shapes=[pltpu.VMEM((32 * STRIDE, 128), F32), pltpu.VMEM((32 * STRIDE, 128), F32)],
        compiler_params=pltpu.CompilerParams(vmem_limit_bytes=8 * MIB),
        cost_estimate=pl.CostEstimate(
            flops=10**9 * 3 * chunks, bytes_accessed=10**6 * (7 + chunks), transcendentals=0
        ),
        name="precondition",
    )(routes, owner, info, *tables, *raws)


def products_kernel(units, placed, shapes, experts, info, route, query_route, train, *rest):
    n_in = len(shapes)
    n_old = 0 if placed is None else len(placed)
    parts, old = rest[:n_in], rest[n_in : n_in + n_old]
    out, held, total = rest[n_in + n_old :]
    blocks = sum(shapes) // 64
    train_rows = train.shape[0]
    at = 0
    for part, r in zip(parts, shapes):
        held[at : at + r, :] = part[...]
        at += r

    def tile(i, unused):
        here = pl.ds(pl.multiple_of(i * TILE, TILE), TILE)
        g = lax.dot_general(held[...], train[here, :], (((1,), (1,)), ((), ())), preferred_element_type=F32)
        there = route[:, here]
        for u in range(blocks):
            first = pl.multiple_of(info[experts + units[u]] * 64, 64)
            want = jnp.concatenate([query_route[pl.ds(first, 64), :]] * (TILE // 128), 1)
            hit = jnp.where(want == there, g[u * 64 : (u + 1) * 64], 0.0)
            total[u * 8 : (u + 1) * 8, here] = jnp.sum(hit.reshape(8, 8, TILE), axis=0)
        return 0

    lax.fori_loop(0, train_rows // TILE, tile, 0)
    row = lax.broadcasted_iota(jnp.int32, (train_rows, 128), 0)
    col = lax.broadcasted_iota(jnp.int32, (train_rows, 128), 1)
    fold = (lax.shift_right_logical(row, 3) == col).astype(BF16)
    x = total[...]
    hi = x.astype(BF16)
    left = x - hi.astype(F32)
    mid = left.astype(BF16)
    low = (left - mid.astype(F32)).astype(BF16)
    y = jnp.dot(jnp.concatenate([hi, mid, low], 0), fold, preferred_element_type=F32)
    n = blocks * 8
    y = y[:n] + y[n : 2 * n] + y[2 * n :]
    if placed is None:
        out[...] = y
        return
    todo = [(y, units)] + list(zip(old, placed))
    for values, names in todo:
        for u, name in enumerate(names):
            first = pl.multiple_of(info[experts + name] * 8, 8)
            out[pl.ds(first, 8), :] = values[u * 8 : (u + 1) * 8]


def products(info, experts, route, query_route, train, parts, units, old=None, placed=None, queries=0):
    shapes = [p.shape[0] for p in parts]
    blocks = sum(shapes) // 64
    train_rows, width = train.shape
    sm = pl.BlockSpec(memory_space=pltpu.SMEM)
    vm = pl.BlockSpec(memory_space=pltpu.VMEM)
    old = list(old or [])
    return pl.pallas_call(
        functools.partial(products_kernel, units, placed, shapes, experts),
        out_shape=jax.ShapeDtypeStruct((queries if placed else blocks * 8, 128), F32),
        in_specs=[sm] + [vm] * (3 + len(parts) + len(old)),
        out_specs=vm,
        scratch_shapes=[
            pltpu.VMEM((sum(shapes), width), BF16),
            pltpu.VMEM((blocks * 8, train_rows), F32),
        ],
        compiler_params=pltpu.CompilerParams(vmem_limit_bytes=14 * MIB),
        cost_estimate=pl.CostEstimate(
            flops=4 * 128 * max(2, blocks) * train_rows * width // 2,
            bytes_accessed=2 * train_rows * width,
            transcendentals=0,
        ),
        name="products",
    )(info, route, query_route, train, *parts, *old)


def tables_of(devices, slots):
    chips = devices // 2
    far = chips // 2
    ring = [2 * z for z in range(far)] + [2 * z + 1 for z in reversed(range(far))]
    spot = [ring.index(c) for c in range(chips)]
    rows = []
    for me in range(devices):
        place = []
        for slot in range(devices * slots):
            rel = (spot[slot // slots // 2] - spot[me // 2]) % chips
            order = chips - 1 if rel == far else 2 * (chips - rel) - 1 if rel > far else 2 * rel
            across = (slot // slots) % 2 != me % 2
            place.append((across * chips + order) * slots + slot % slots)
        near = []
        for d in range(far + 1):
            for core in (me % 2, 1 - me % 2):
                chip = ring[(spot[me // 2] + (d if core else -d)) % chips]
                near += [2 * chip + core, 2 * chip + 1 - core]
        rows.append(place + near)
    return ring, np.array(rows, np.int32)


def tie(value, other):
    return lax.optimization_barrier((value, other))[0]


def local(
    query_grads,
    query_routes,
    train_grads,
    train_routes,
    train_counts,
    owner_slot,
    basis_s,
    basis_a,
    eigenvalues,
):
    devices = lax.axis_size("shard")
    me = lax.axis_index("shard")
    experts = owner_slot.shape[0]
    queries, top = query_routes.shape
    width = query_grads.shape[2]
    train_dev = train_grads.shape[0]
    slots = basis_s.shape[0]
    chips = devices // 2
    far = chips // 2
    ring, constants = tables_of(devices, slots)
    info = lax.dynamic_index_in_dim(jnp.asarray(constants), me, 0, keepdims=False)

    def shift(steps):
        return [
            (2 * c + k, 2 * ring[(i + steps[k]) % chips] + k) for i, c in enumerate(ring) for k in (0, 1)
        ]

    ahead, back, stream = shift((1, 1)), shift((-1, -1)), shift((1, -1))
    across = [(d, d ^ 1) for d in range(devices)]
    send = lambda v, way: lax.ppermute(v, "shard", way)

    raw = query_grads.transpose(1, 0, 2).reshape(-1, width)
    other_raw = send(raw, across)

    pack = pack_factors(basis_s, basis_a, eigenvalues)
    got, up, down = [pack], pack, pack
    cut = pack.shape[0] // 2
    for step in range(1, far + 1):
        if step == far:
            up, down = up[:cut], down[cut:]
            raw, up = tie(raw, got[-1]), tie(up, other_raw)
        up, down = send(up, ahead), send(down, back)
        got += [up, down]
    a = send(raw, stream)
    mine = jnp.concatenate(got, axis=0)
    sib = send(mine, across)
    tables = prepare(sib, experts, experts // 2, prepare(mine, experts, 0))

    live = jnp.arange(train_dev, dtype=jnp.int32) < train_counts[0]
    route = jnp.where(live[:, None], train_routes, -1).reshape(1, train_dev * top)
    train = train_grads.reshape(train_dev * top, width)
    query_route = query_routes.reshape(devices, 8, top).transpose(0, 2, 1).reshape(queries * top, 1)
    query_route = jnp.broadcast_to(query_route, (queries * top, 128))

    pre = lambda raws, names: precondition(query_routes, owner_slot, info, tables, raws, names)
    multiply = lambda parts, names, **more: products(
        info, experts, route, query_route, train, parts, names, **more
    )
    (b,) = pre([other_raw], [1])
    held, names = [send(b, across), b], [0, 1]
    (a,) = pre([tie(a, b)], [4])
    b = send(b, stream)
    done, placed = [], []
    for step in range(1, far):
        if done:
            a = tie(a, done[-1])
        next_a = send(a, stream)
        held += [a, send(a, across)]
        if step < far - 1:
            next_b = send(b, stream)
        held += [b, send(b, across)]
        names += [4 * step, 4 * step + 2, 4 * step + 1, 4 * step + 3]
        a, b = next_a, next_b
        if step > 1 or far < 4:
            pass
        done.append(multiply(held, names))
        placed.append(names)
        held, names = [], []
    if done:
        a = tie(a, done[-1])
    return multiply([a, send(a, across)], [4 * far, 4 * far + 2], old=done, placed=placed, queries=queries)


def solution(mesh):
    placed = (
        P(("groups", "shard"), None, None),
        P("groups", None),
        P(("groups", "shard"), None, None),
        P(("groups", "shard"), None),
        P(("groups", "shard")),
        P(),
        P("shard", None, None),
        P("shard", None, None),
        P("shard", None, None),
    )
    return jax.shard_map(
        local, mesh=mesh, in_specs=placed, out_specs=P("groups", "shard"), check_vma=False
    )
```

```python
import functools

import jax
import jax.numpy as jnp
import numpy as np
from jax import lax
from jax.experimental import pallas as pl
from jax.experimental.pallas import tpu as pltpu
from jax.sharding import PartitionSpec as P

DAMPING = 0.01
F32, BF16 = jnp.float32, jnp.bfloat16
STRIDE = 65
GROUP = 64
TILE = 512
MIB = 2**20


def split(x):
    hi = x.astype(BF16)
    return hi, (x - hi.astype(F32)).astype(BF16)


def swap(x):
    return pltpu.roll(x, 64, 1)


def prepare_kernel(at, count, src, *rest):
    tab_a, tab_at, tab_s, tab_st, scale = rest[-5:]
    left64 = lax.broadcasted_iota(jnp.int32, (64, 128), 1) < 64

    def both(pair, unused):
        e = 2 * pair
        base = pl.multiple_of(pair * 192, 192)
        f_s = jnp.concatenate([src[pl.ds(base + h, 32, stride=2), :] for h in (0, 1)], 0)
        f_a = src[pl.ds(base + 64, 64), :]
        f_l = src[pl.ds(base + 128, 64), :]

        def twice(f):
            r = swap(f)
            return jnp.where(left64, f, r), jnp.where(left64, r, f)

        for w0, (s, a, lam) in enumerate(zip(twice(f_s), twice(f_a), twice(f_l))):
            to = at + e + w0
            scale[to] = 1.0 / (lam + DAMPING)
            t = jnp.concatenate([s, a], 0).T[:64]
            r = swap(t)
            st, a_t = jnp.where(left64, t, r), jnp.where(left64, r, t)
            for ref, m in ((tab_s, s), (tab_st, st)):
                hi, lo = split(m)
                ref[to, :, :128] = hi
                ref[to, :, 128:] = lo
            for ref, m in ((tab_a, a), (tab_at, a_t)):
                for w in (0, 1):
                    hi, lo = split(jnp.where(left64 if w == 0 else ~left64, m, 0.0))
                    ref[to, w, :64] = hi
                    ref[to, w, 64:] = lo
        return 0

    lax.fori_loop(0, count // 2, both, 0, unroll=2)


def prepare(src, experts, at, tables=()):
    vm = pl.BlockSpec(memory_space=pltpu.VMEM)
    return pl.pallas_call(
        functools.partial(prepare_kernel, at, experts // 2),
        out_shape=[
            jax.ShapeDtypeStruct((experts, 2, 128, 128), BF16),
            jax.ShapeDtypeStruct((experts, 2, 128, 128), BF16),
            jax.ShapeDtypeStruct((experts, 64, 256), BF16),
            jax.ShapeDtypeStruct((experts, 64, 256), BF16),
            jax.ShapeDtypeStruct((experts, 64, 128), F32),
        ],
        in_specs=[vm] * (1 + len(tables)),
        out_specs=[vm] * 5,
        input_output_aliases={1 + i: i for i in range(len(tables))},
        compiler_params=pltpu.CompilerParams(vmem_limit_bytes=4 * MIB),
        cost_estimate=pl.CostEstimate(flops=1000, bytes_accessed=1000, transcendentals=0),
        name="prepare",
    )(src, *tables)


def pack_kernel(s, a, lam, out, held, sems):
    copies = [pltpu.make_async_copy(m, held.at[i], sems.at[i]) for i, m in enumerate((s, a, lam))]
    for copy in copies:
        copy.start()
    for i, copy in enumerate(copies):
        copy.wait()
        for p in range(s.shape[0] // 2):
            first = (3 * p + i) * 64
            out[first : first + 64, :] = jnp.concatenate([held[i, 2 * p], held[i, 2 * p + 1]], axis=1)


def pack_factors(*factors):
    slots = factors[0].shape[0]
    return pl.pallas_call(
        pack_kernel,
        out_shape=jax.ShapeDtypeStruct((slots * 96, 128), F32),
        in_specs=[pl.BlockSpec(memory_space=pltpu.HBM)] * 3,
        out_specs=pl.BlockSpec(memory_space=pltpu.VMEM),
        scratch_shapes=[pltpu.VMEM((3, slots, 64, 64), F32), pltpu.SemaphoreType.DMA((3,))],
        compiler_params=pltpu.CompilerParams(vmem_limit_bytes=4 * MIB),
        cost_estimate=pl.CostEstimate(flops=1000, bytes_accessed=1000, transcendentals=0),
        name="pack",
    )(*[pltpu.with_memory_space_constraint(m, pltpu.HBM) for m in factors])


def precondition_kernel(units, routes, owner, info, tab_a, tab_at, tab_s, tab_st, scale, *rest):
    chunks = len(units)
    experts = owner.shape[0]
    raws, outs = rest[:chunks], rest[chunks : 2 * chunks]
    xs, ys = rest[2 * chunks :]
    left64 = lax.broadcasted_iota(jnp.int32, (64, 128), 1) < 64
    left = left64[:32]

    def pair(tab, e1, e2, three):
        hi = [tab[e1, 0, :64], tab[e2, 1, :64]]
        lo = [tab[e1, 0, 64:], tab[e2, 1, 64:]]
        return jnp.concatenate(hi + (hi if three else []) + lo, 0)

    def cross(tab, e1, e2, x):
        hi, lo = split(x)
        o = jnp.dot(
            jnp.concatenate([tab[e1], tab[e2]], 0),
            jnp.concatenate([hi, lo, hi, lo], 0),
            preferred_element_type=F32,
        )
        return jnp.where(left64, o[:64], o[64:])

    for ch in range(chunks):
        raw, out = raws[ch], outs[ch]
        first = info[experts + units[ch]] * 8
        for c in range(32):
            xs[pl.ds(c * STRIDE, 64), :] = raw[:, c * 128 : (c + 1) * 128].astype(F32)

        def group(b, unused):
            es, g, x = [], [], []
            for i in range(GROUP):
                row = b * GROUP + i
                es.append(info[owner[routes[first + row % 8, row // 8]]])
                g.append(xs[pl.ds(row, 32, stride=STRIDE), :])
            n = GROUP // 2
            ee = [(es[2 * p], es[2 * p + 1]) for p in range(n)]
            for p in range(n):
                g1, g2 = g[2 * p], g[2 * p + 1]
                h = [jnp.where(left, g1, swap(g2)), jnp.where(left, swap(g1), g2)]
                h = jnp.concatenate(h, 0).astype(BF16)
                h = jnp.concatenate([h, h], 1)
                x.append(jnp.dot(h, pair(tab_a, *ee[p], False), preferred_element_type=F32))
            x = [
                cross(tab_st, *ee[p], x[p]) * jnp.where(left64, scale[ee[p][0]], scale[ee[p][1]])
                for p in range(n)
            ]
            x = [cross(tab_s, *ee[p], x[p]) for p in range(n)]
            for p in range(n):
                hi, lo = split(x[p])
                h = jnp.concatenate([hi, lo, hi], 1)
                y = jnp.dot(h, pair(tab_at, *ee[p], True), preferred_element_type=F32)
                top, low = y[:32], y[32:]
                for w, v in enumerate((jnp.where(left, top, swap(low)), jnp.where(left, swap(top), low))):
                    row = b * GROUP + 2 * p + w
                    ys[pl.ds(row, 32, stride=STRIDE), :] = v
            return 0

        lax.fori_loop(0, 64 // GROUP, group, 0)
        for c in range(32):
            out[:, c * 128 : (c + 1) * 128] = ys[pl.ds(c * STRIDE, 64), :].astype(BF16)


def precondition(routes, owner, info, tables, raws, units):
    chunks = len(units)
    sm = pl.BlockSpec(memory_space=pltpu.SMEM)
    vm = pl.BlockSpec(memory_space=pltpu.VMEM)
    return pl.pallas_call(
        functools.partial(precondition_kernel, units),
        out_shape=[jax.ShapeDtypeStruct((64, raws[0].shape[1]), BF16)] * chunks,
        in_specs=[sm] * 3 + [vm] * (5 + len(raws)),
        out_specs=[vm] * chunks,
        scratch_shapes=[pltpu.VMEM((32 * STRIDE, 128), F32), pltpu.VMEM((32 * STRIDE, 128), F32)],
        compiler_params=pltpu.CompilerParams(vmem_limit_bytes=8 * MIB),
        cost_estimate=pl.CostEstimate(flops=1000, bytes_accessed=1000, transcendentals=0),
        name="precondition",
    )(routes, owner, info, *tables, *raws)


def products_kernel(units, placed, shapes, experts, info, route, query_route, train, *rest):
    n_in = len(shapes)
    n_old = 0 if placed is None else len(placed)
    parts, old = rest[:n_in], rest[n_in : n_in + n_old]
    out, held, total = rest[n_in + n_old :]
    blocks = sum(shapes) // 64
    train_rows = train.shape[0]
    at = 0
    for part, r in zip(parts, shapes):
        held[at : at + r, :] = part[...]
        at += r

    def tile(i, unused):
        here = pl.ds(pl.multiple_of(i * TILE, TILE), TILE)
        g = lax.dot_general(held[...], train[here, :], (((1,), (1,)), ((), ())), preferred_element_type=F32)
        there = route[:, here]
        for u in range(blocks):
            first = pl.multiple_of(info[experts + units[u]] * 64, 64)
            want = jnp.concatenate([query_route[pl.ds(first, 64), :]] * (TILE // 128), 1)
            hit = jnp.where(want == there, g[u * 64 : (u + 1) * 64], 0.0)
            total[u * 8 : (u + 1) * 8, here] = jnp.sum(hit.reshape(8, 8, TILE), axis=0)
        return 0

    lax.fori_loop(0, train_rows // TILE, tile, 0)
    row = lax.broadcasted_iota(jnp.int32, (train_rows, 128), 0)
    col = lax.broadcasted_iota(jnp.int32, (train_rows, 128), 1)
    fold = (lax.shift_right_logical(row, 3) == col).astype(BF16)
    x = total[...]
    hi = x.astype(BF16)
    left = x - hi.astype(F32)
    mid = left.astype(BF16)
    low = (left - mid.astype(F32)).astype(BF16)
    y = jnp.dot(jnp.concatenate([hi, mid, low], 0), fold, preferred_element_type=F32)
    n = blocks * 8
    y = y[:n] + y[n : 2 * n] + y[2 * n :]
    if placed is None:
        out[...] = y
        return
    todo = [(y, units)] + list(zip(old, placed))
    for values, names in todo:
        for u, name in enumerate(names):
            first = pl.multiple_of(info[experts + name] * 8, 8)
            out[pl.ds(first, 8), :] = values[u * 8 : (u + 1) * 8]


def products(info, experts, route, query_route, train, parts, units, old=None, placed=None, queries=0):
    shapes = [p.shape[0] for p in parts]
    blocks = sum(shapes) // 64
    train_rows, width = train.shape
    sm = pl.BlockSpec(memory_space=pltpu.SMEM)
    vm = pl.BlockSpec(memory_space=pltpu.VMEM)
    old = list(old or [])
    return pl.pallas_call(
        functools.partial(products_kernel, units, placed, shapes, experts),
        out_shape=jax.ShapeDtypeStruct((queries if placed else blocks * 8, 128), F32),
        in_specs=[sm] + [vm] * (3 + len(parts) + len(old)),
        out_specs=vm,
        scratch_shapes=[
            pltpu.VMEM((sum(shapes), width), BF16),
            pltpu.VMEM((blocks * 8, train_rows), F32),
        ],
        compiler_params=pltpu.CompilerParams(vmem_limit_bytes=14 * MIB),
        cost_estimate=pl.CostEstimate(flops=1000, bytes_accessed=1000, transcendentals=0),
        name="products",
    )(info, route, query_route, train, *parts, *old)


def tables_of(devices, slots):
    chips = devices // 2
    far = chips // 2
    ring = [2 * z for z in range(far)] + [2 * z + 1 for z in reversed(range(far))]
    spot = [ring.index(c) for c in range(chips)]
    rows = []
    for me in range(devices):
        place = []
        for slot in range(devices * slots):
            rel = (spot[slot // slots // 2] - spot[me // 2]) % chips
            order = chips - 1 if rel == far else 2 * (chips - rel) - 1 if rel > far else 2 * rel
            across = (slot // slots) % 2 != me % 2
            place.append((across * chips + order) * slots + slot % slots)
        near = []
        for d in range(far + 1):
            for core in (me % 2, 1 - me % 2):
                chip = ring[(spot[me // 2] + (d if core else -d)) % chips]
                near += [2 * chip + core, 2 * chip + 1 - core]
        rows.append(place + near)
    return ring, np.array(rows, np.int32)


def tie(value, other):
    return lax.optimization_barrier((value, other))[0]


def local(
    query_grads,
    query_routes,
    train_grads,
    train_routes,
    train_counts,
    owner_slot,
    basis_s,
    basis_a,
    eigenvalues,
):
    devices = lax.axis_size("shard")
    me = lax.axis_index("shard")
    experts = owner_slot.shape[0]
    queries, top = query_routes.shape
    width = query_grads.shape[2]
    train_dev = train_grads.shape[0]
    slots = basis_s.shape[0]
    chips = devices // 2
    far = chips // 2
    ring, constants = tables_of(devices, slots)
    info = lax.dynamic_index_in_dim(jnp.asarray(constants), me, 0, keepdims=False)

    def shift(steps):
        return [
            (2 * c + k, 2 * ring[(i + steps[k]) % chips] + k) for i, c in enumerate(ring) for k in (0, 1)
        ]

    ahead, back, stream = shift((1, 1)), shift((-1, -1)), shift((1, -1))
    across = [(d, d ^ 1) for d in range(devices)]
    send = lambda v, way: lax.ppermute(v, "shard", way)

    raw = query_grads.transpose(1, 0, 2).reshape(-1, width)
    other_raw = send(raw, across)

    live = jnp.arange(train_dev, dtype=jnp.int32) < train_counts[0]
    route = jnp.where(live[:, None], train_routes, -1).reshape(1, train_dev * top)
    train = train_grads.reshape(train_dev * top, width)
    query_route = query_routes.reshape(devices, 8, top).transpose(0, 2, 1).reshape(queries * top, 1)
    query_route = jnp.broadcast_to(query_route, (queries * top, 128))

    pack = pack_factors(basis_s, basis_a, eigenvalues)
    got, up, down = [pack], pack, pack
    cut = pack.shape[0] // 2
    for step in range(1, far + 1):
        if step == 3:
            up = tie(up, (other_raw, info, route, query_route))
        if step == far:
            up, down = up[:cut], down[cut:]
            raw = tie(raw, got[-1])
        up, down = send(up, ahead), send(down, back)
        got += [up, down]
    a = send(raw, stream)
    mine = jnp.concatenate(got, axis=0)
    sib = send(mine, across)
    tables = prepare(sib, experts, experts // 2, prepare(mine, experts, 0))

    pre = lambda *args: precondition(query_routes, owner_slot, info, tables, *args)
    (b,) = pre([other_raw], [1])
    held, names = [send(b, across), b], [0, 1]
    (a,) = pre([tie(a, b)], [4])
    b = send(b, stream)
    multiply = lambda parts, names, **more: products(
        info, experts, route, query_route, train, parts, names, **more
    )
    held += [a, send(a, across)]
    names += [4, 6]
    done, placed = [], []
    coming = [(b, 5), (send(a, stream), 8)]
    while len(coming) > 1 or coming[0][1] < 4 * far:
        (now, name), (after, after_name) = coming
        if name // 4 < far - 1:
            further = [(send(now, stream), name + 4)]
        else:
            further = [(send(now, stream), 4 * far)] if name % 4 == 0 else []
        held[0] = tie(held[0], now)
        done.append(multiply(held, names))
        placed.append(names)
        held, names = [now, send(now, across)], [name, name + 2]
        coming = [(tie(after, done[-1]), after_name)] + further
    now, name = coming[0]
    held += [now, send(now, across)]
    return multiply(held, names + [name, name + 2], old=done, placed=placed, queries=queries)


def solution(mesh):
    placed = (
        P(("groups", "shard"), None, None),
        P("groups", None),
        P(("groups", "shard"), None, None),
        P(("groups", "shard"), None),
        P(("groups", "shard")),
        P(),
        P("shard", None, None),
        P("shard", None, None),
        P("shard", None, None),
    )
    return jax.shard_map(
        local, mesh=mesh, in_specs=placed, out_specs=P("groups", "shard"), check_vma=False
    )
```

```python
import functools

import jax
import jax.numpy as jnp
import numpy as np
from jax import lax
from jax.experimental import pallas as pl
from jax.experimental.pallas import tpu as pltpu
from jax.sharding import PartitionSpec as P

DAMPING = 0.01
F32, BF16 = jnp.float32, jnp.bfloat16
STRIDE = 65
GROUP = 64
TILE = 512
MIB = 2**20


def split(x):
    hi = x.astype(BF16)
    return hi, (x - hi.astype(F32)).astype(BF16)


def swap(x):
    return pltpu.roll(x, 64, 1)


def prepare_kernel(at, count, src, *rest):
    tab_a, tab_at, tab_s, tab_st, scale = rest[-5:]
    left64 = lax.broadcasted_iota(jnp.int32, (64, 128), 1) < 64

    def both(pair, unused):
        e = 2 * pair
        base = pl.multiple_of(pair * 192, 192)
        f_s = jnp.concatenate([src[pl.ds(base + h, 32, stride=2), :] for h in (0, 1)], 0)
        f_a = src[pl.ds(base + 64, 64), :]
        f_l = src[pl.ds(base + 128, 64), :]

        def twice(f):
            r = swap(f)
            return jnp.where(left64, f, r), jnp.where(left64, r, f)

        for w0, (s, a, lam) in enumerate(zip(twice(f_s), twice(f_a), twice(f_l))):
            to = at + e + w0
            scale[to] = 1.0 / (lam + DAMPING)
            t = jnp.concatenate([s, a], 0).T[:64]
            r = swap(t)
            st, a_t = jnp.where(left64, t, r), jnp.where(left64, r, t)
            for ref, m in ((tab_s, s), (tab_st, st)):
                hi, lo = split(m)
                ref[to, :, :128] = hi
                ref[to, :, 128:] = lo
            for ref, m in ((tab_a, a), (tab_at, a_t)):
                for w in (0, 1):
                    hi, lo = split(jnp.where(left64 if w == 0 else ~left64, m, 0.0))
                    ref[to, w, :64] = hi
                    ref[to, w, 64:] = lo
        return 0

    lax.fori_loop(0, count // 2, both, 0, unroll=2)


def prepare(src, experts, at, tables=()):
    vm = pl.BlockSpec(memory_space=pltpu.VMEM)
    return pl.pallas_call(
        functools.partial(prepare_kernel, at, src.shape[0] // 96),
        out_shape=[
            jax.ShapeDtypeStruct((experts, 2, 128, 128), BF16),
            jax.ShapeDtypeStruct((experts, 2, 128, 128), BF16),
            jax.ShapeDtypeStruct((experts, 64, 256), BF16),
            jax.ShapeDtypeStruct((experts, 64, 256), BF16),
            jax.ShapeDtypeStruct((experts, 64, 128), F32),
        ],
        in_specs=[vm] * (1 + len(tables)),
        out_specs=[vm] * 5,
        input_output_aliases={1 + i: i for i in range(len(tables))},
        compiler_params=pltpu.CompilerParams(vmem_limit_bytes=4 * MIB),
        cost_estimate=pl.CostEstimate(flops=1000, bytes_accessed=1000, transcendentals=0),
        name="prepare",
    )(src, *tables)


def pack_kernel(s, a, lam, out, held, sems):
    copies = [pltpu.make_async_copy(m, held.at[i], sems.at[i]) for i, m in enumerate((s, a, lam))]
    for copy in copies:
        copy.start()
    for i, copy in enumerate(copies):
        copy.wait()
        for p in range(s.shape[0] // 2):
            first = (3 * p + i) * 64
            out[first : first + 64, :] = jnp.concatenate([held[i, 2 * p], held[i, 2 * p + 1]], axis=1)


def pack_factors(*factors):
    slots = factors[0].shape[0]
    return pl.pallas_call(
        pack_kernel,
        out_shape=jax.ShapeDtypeStruct((slots * 96, 128), F32),
        in_specs=[pl.BlockSpec(memory_space=pltpu.HBM)] * 3,
        out_specs=pl.BlockSpec(memory_space=pltpu.VMEM),
        scratch_shapes=[pltpu.VMEM((3, slots, 64, 64), F32), pltpu.SemaphoreType.DMA((3,))],
        compiler_params=pltpu.CompilerParams(vmem_limit_bytes=4 * MIB),
        cost_estimate=pl.CostEstimate(flops=1000, bytes_accessed=1000, transcendentals=0),
        name="pack",
    )(*[pltpu.with_memory_space_constraint(m, pltpu.HBM) for m in factors])


def precondition_kernel(units, routes, owner, info, tab_a, tab_at, tab_s, tab_st, scale, *rest):
    chunks = len(units)
    experts = owner.shape[0]
    raws, outs = rest[:chunks], rest[chunks : 2 * chunks]
    xs, ys = rest[2 * chunks :]
    left64 = lax.broadcasted_iota(jnp.int32, (64, 128), 1) < 64
    left = left64[:32]

    def pair(tab, e1, e2, three):
        hi = [tab[e1, 0, :64], tab[e2, 1, :64]]
        lo = [tab[e1, 0, 64:], tab[e2, 1, 64:]]
        return jnp.concatenate(hi + (hi if three else []) + lo, 0)

    def cross(tab, e1, e2, x):
        hi, lo = split(x)
        o = jnp.dot(
            jnp.concatenate([tab[e1], tab[e2]], 0),
            jnp.concatenate([hi, lo, hi, lo], 0),
            preferred_element_type=F32,
        )
        return jnp.where(left64, o[:64], o[64:])

    for ch in range(chunks):
        raw, out = raws[ch], outs[ch]
        first = info[experts + units[ch]] * 8
        for c in range(32):
            xs[pl.ds(c * STRIDE, 64), :] = raw[:, c * 128 : (c + 1) * 128].astype(F32)

        def group(b, unused):
            es, g, x = [], [], []
            for i in range(GROUP):
                row = b * GROUP + i
                es.append(info[owner[routes[first + row // 8, row % 8]]])
                g.append(xs[pl.ds(row, 32, stride=STRIDE), :])
            n = GROUP // 2
            ee = [(es[2 * p], es[2 * p + 1]) for p in range(n)]
            for p in range(n):
                g1, g2 = g[2 * p], g[2 * p + 1]
                h = [jnp.where(left, g1, swap(g2)), jnp.where(left, swap(g1), g2)]
                h = jnp.concatenate(h, 0).astype(BF16)
                h = jnp.concatenate([h, h], 1)
                x.append(jnp.dot(h, pair(tab_a, *ee[p], False), preferred_element_type=F32))
            x = [
                cross(tab_st, *ee[p], x[p]) * jnp.where(left64, scale[ee[p][0]], scale[ee[p][1]])
                for p in range(n)
            ]
            x = [cross(tab_s, *ee[p], x[p]) for p in range(n)]
            for p in range(n):
                hi, lo = split(x[p])
                h = jnp.concatenate([hi, lo, hi], 1)
                y = jnp.dot(h, pair(tab_at, *ee[p], True), preferred_element_type=F32)
                top, low = y[:32], y[32:]
                for w, v in enumerate((jnp.where(left, top, swap(low)), jnp.where(left, swap(top), low))):
                    row = b * GROUP + 2 * p + w
                    ys[pl.ds((row % 8) * 8 + row // 8, 32, stride=STRIDE), :] = v
            return 0

        lax.fori_loop(0, 64 // GROUP, group, 0)
        for c in range(32):
            out[:, c * 128 : (c + 1) * 128] = ys[pl.ds(c * STRIDE, 64), :].astype(BF16)


def precondition(routes, owner, info, tables, raws, units):
    chunks = len(units)
    sm = pl.BlockSpec(memory_space=pltpu.SMEM)
    vm = pl.BlockSpec(memory_space=pltpu.VMEM)
    return pl.pallas_call(
        functools.partial(precondition_kernel, units),
        out_shape=[jax.ShapeDtypeStruct((64, raws[0].shape[1]), BF16)] * chunks,
        in_specs=[sm] * 3 + [vm] * (5 + len(raws)),
        out_specs=[vm] * chunks,
        scratch_shapes=[pltpu.VMEM((32 * STRIDE, 128), F32), pltpu.VMEM((32 * STRIDE, 128), F32)],
        compiler_params=pltpu.CompilerParams(vmem_limit_bytes=8 * MIB),
        cost_estimate=pl.CostEstimate(flops=1000, bytes_accessed=1000, transcendentals=0),
        name="precondition",
    )(routes, owner, info, *tables, *raws)


def products_kernel(units, placed, shapes, experts, info, route, query_route, train, *rest):
    n_in = len(shapes)
    n_old = 0 if placed is None else len(placed)
    parts, old = rest[:n_in], rest[n_in : n_in + n_old]
    out, held, total = rest[n_in + n_old :]
    blocks = sum(shapes) // 64
    train_rows = train.shape[0]
    at = 0
    for part, r in zip(parts, shapes):
        held[at : at + r, :] = part[...]
        at += r

    def tile(i, unused):
        here = pl.ds(pl.multiple_of(i * TILE, TILE), TILE)
        g = lax.dot_general(held[...], train[here, :], (((1,), (1,)), ((), ())), preferred_element_type=F32)
        there = route[:, here]
        for u in range(blocks):
            first = pl.multiple_of(info[experts + units[u]] * 64, 64)
            want = jnp.concatenate([query_route[pl.ds(first, 64), :]] * (TILE // 128), 1)
            hit = jnp.where(want == there, g[u * 64 : (u + 1) * 64], 0.0)
            total[u * 8 : (u + 1) * 8, here] = jnp.sum(hit.reshape(8, 8, TILE), axis=0)
        return 0

    lax.fori_loop(0, train_rows // TILE, tile, 0)
    row = lax.broadcasted_iota(jnp.int32, (train_rows, 128), 0)
    col = lax.broadcasted_iota(jnp.int32, (train_rows, 128), 1)
    fold = (lax.shift_right_logical(row, 3) == col).astype(BF16)
    x = total[...]
    hi = x.astype(BF16)
    left = x - hi.astype(F32)
    mid = left.astype(BF16)
    low = (left - mid.astype(F32)).astype(BF16)
    y = jnp.dot(jnp.concatenate([hi, mid, low], 0), fold, preferred_element_type=F32)
    n = blocks * 8
    y = y[:n] + y[n : 2 * n] + y[2 * n :]
    if placed is None:
        out[...] = y
        return
    todo = [(y, units)] + list(zip(old, placed))
    for values, names in todo:
        for u, name in enumerate(names):
            first = pl.multiple_of(info[experts + name] * 8, 8)
            out[pl.ds(first, 8), :] = values[u * 8 : (u + 1) * 8]


def products(info, experts, route, query_route, train, parts, units, old=None, placed=None, queries=0):
    shapes = [p.shape[0] for p in parts]
    blocks = sum(shapes) // 64
    train_rows, width = train.shape
    sm = pl.BlockSpec(memory_space=pltpu.SMEM)
    vm = pl.BlockSpec(memory_space=pltpu.VMEM)
    old = list(old or [])
    return pl.pallas_call(
        functools.partial(products_kernel, units, placed, shapes, experts),
        out_shape=jax.ShapeDtypeStruct((queries if placed else blocks * 8, 128), F32),
        in_specs=[sm] + [vm] * (3 + len(parts) + len(old)),
        out_specs=vm,
        scratch_shapes=[
            pltpu.VMEM((sum(shapes), width), BF16),
            pltpu.VMEM((blocks * 8, train_rows), F32),
        ],
        compiler_params=pltpu.CompilerParams(vmem_limit_bytes=14 * MIB),
        cost_estimate=pl.CostEstimate(flops=1000, bytes_accessed=1000, transcendentals=0),
        name="products",
    )(info, route, query_route, train, *parts, *old)


def tables_of(devices, slots):
    chips = devices // 2
    far = chips // 2
    ring = [2 * z for z in range(far)] + [2 * z + 1 for z in reversed(range(far))]
    spot = [ring.index(c) for c in range(chips)]
    rows = []
    for me in range(devices):
        place = []
        for slot in range(devices * slots):
            rel = (spot[slot // slots // 2] - spot[me // 2]) % chips
            order = chips - 1 if rel == far else 2 * (chips - rel) - 1 if rel > far else 2 * rel
            across = (slot // slots) % 2 != me % 2
            place.append((across * chips + order) * slots + slot % slots)
        near = []
        for d in range(far + 1):
            for core in (me % 2, 1 - me % 2):
                chip = ring[(spot[me // 2] + (d if core else -d)) % chips]
                near += [2 * chip + core, 2 * chip + 1 - core]
        rows.append(place + near)
    return ring, np.array(rows, np.int32)


def tie(value, other):
    return lax.optimization_barrier((value, other))[0]


def local(
    query_grads,
    query_routes,
    train_grads,
    train_routes,
    train_counts,
    owner_slot,
    basis_s,
    basis_a,
    eigenvalues,
):
    devices = lax.axis_size("shard")
    me = lax.axis_index("shard")
    experts = owner_slot.shape[0]
    queries, top = query_routes.shape
    width = query_grads.shape[2]
    train_dev = train_grads.shape[0]
    slots = basis_s.shape[0]
    chips = devices // 2
    far = chips // 2
    ring, constants = tables_of(devices, slots)
    info = lax.dynamic_index_in_dim(jnp.asarray(constants), me, 0, keepdims=False)

    def shift(steps):
        return [
            (2 * c + k, 2 * ring[(i + steps[k]) % chips] + k) for i, c in enumerate(ring) for k in (0, 1)
        ]

    ahead, back, stream = shift((1, 1)), shift((-1, -1)), shift((1, -1))
    across = [(d, d ^ 1) for d in range(devices)]
    send = lambda v, way: lax.ppermute(v, "shard", way)

    raw = query_grads.reshape(-1, width)
    other_raw = send(raw, across)

    live = jnp.arange(train_dev, dtype=jnp.int32) < train_counts[0]
    route = jnp.where(live[:, None], train_routes, -1).reshape(1, train_dev * top)
    train = train_grads.reshape(train_dev * top, width)
    query_route = query_routes.reshape(devices, 8, top).transpose(0, 2, 1).reshape(queries * top, 1)
    query_route = jnp.broadcast_to(query_route, (queries * top, 128))

    pack = pack_factors(basis_s, basis_a, eigenvalues)
    cut = pack.shape[0] // 2
    ahead2, back2 = shift((2, 2)), shift((-2, -2))
    got, up, down, tables, crossed = [pack], pack, pack, (), 0
    for first in range(1, far, 2):
        if first == 3:
            up = tie(up, (other_raw, info, route, query_route))
        got += [send(up, ahead), send(down, back)]
        if first + 1 == far:
            got += [send(up[:cut], ahead2), send(down[cut:], back2)]
        else:
            up, down = send(up, ahead2), send(down, back2)
            got += [up, down]
        if first > 1 and first + 1 < far:
            continue
        mine = jnp.concatenate(got, axis=0)
        sib = send(mine, across)
        tables = prepare(mine, experts, crossed, tables)
        tables = prepare(sib, experts, experts // 2 + crossed, tables)
        crossed += mine.shape[0] // 96
        got = []
    near = send(tie(raw, up), stream)
    next_near = send(near, stream)

    pre = lambda *args: precondition(query_routes, owner_slot, info, tables, *args)
    (b,) = pre([tie(other_raw, near)], [1])
    queue = [([send(b, across), b], [0, 1])]
    (a,) = pre([tie(next_near, b)], [8])
    b = send(b, stream)
    later = ([a, send(a, across)], [8, 10])
    multiply = lambda parts, names, **more: products(
        info, experts, route, query_route, train, parts, names, **more
    )
    done, placed = [], []
    coming = [(b, 5), (send(a, stream), 12)]
    while len(coming) > 1:
        (now, name), (after, after_name) = coming
        last = 4 * far if name % 4 == 0 else 4 * far - 3
        further = [(send(now, stream), name + 4)] if name < last else []
        if name == 5:
            (a,) = pre([tie(near, now)], [4])
            queue += [([a, send(a, across)], [4, 6]), later]
            barrier = a
        else:
            parts, names = [], []
            for p, n in queue[:2]:
                parts, names = parts + p, names + n
            parts[0] = tie(parts[0], now)
            barrier = multiply(parts, names)
            done.append(barrier)
            placed.append(names)
            queue = queue[2:]
        queue.append(([now, send(now, across)], [name, name + 2]))
        coming = [(tie(after, barrier), after_name)] + further
    now, name = coming[0]
    queue.append(([now, send(now, across)], [name, name + 2]))
    parts, names = [], []
    for p, n in queue:
        parts, names = parts + p, names + n
    return multiply(parts, names, old=done, placed=placed, queries=queries)


def solution(mesh):
    placed = (
        P(("groups", "shard"), None, None),
        P("groups", None),
        P(("groups", "shard"), None, None),
        P(("groups", "shard"), None),
        P(("groups", "shard")),
        P(),
        P("shard", None, None),
        P("shard", None, None),
        P("shard", None, None),
    )
    return jax.shard_map(
        local, mesh=mesh, in_specs=placed, out_specs=P("groups", "shard"), check_vma=False
    )
```

```python
import functools

import jax
import jax.numpy as jnp
import numpy as np
from jax import lax
from jax.experimental import pallas as pl
from jax.experimental.pallas import tpu as pltpu
from jax.sharding import PartitionSpec as P

DAMPING = 0.01
F32, BF16 = jnp.float32, jnp.bfloat16
STRIDE = 65
GROUP = 64
TILE = 1024
MIB = 2**20


def split(x):
    hi = x.astype(BF16)
    return hi, (x - hi.astype(F32)).astype(BF16)


def swap(x):
    return pltpu.roll(x, 64, 1)


def prepare_kernel(at, count, src, *rest):
    tab_a, tab_at, tab_s, tab_st, scale = rest[-5:]
    left64 = lax.broadcasted_iota(jnp.int32, (64, 128), 1) < 64

    def both(pair, unused):
        e = 2 * pair
        base = pl.multiple_of(pair * 192, 192)
        f_s = jnp.concatenate([src[pl.ds(base + h, 32, stride=2), :] for h in (0, 1)], 0)
        f_a = src[pl.ds(base + 64, 64), :]
        f_l = src[pl.ds(base + 128, 64), :]

        def twice(f):
            r = swap(f)
            return jnp.where(left64, f, r), jnp.where(left64, r, f)

        for w0, (s, a, lam) in enumerate(zip(twice(f_s), twice(f_a), twice(f_l))):
            to = at + e + w0
            scale[to] = 1.0 / (lam + DAMPING)
            t = jnp.concatenate([s, a], 0).T[:64]
            r = swap(t)
            st, a_t = jnp.where(left64, t, r), jnp.where(left64, r, t)
            for ref, m in ((tab_s, s), (tab_st, st)):
                hi, lo = split(m)
                ref[to, :, :128] = hi
                ref[to, :, 128:] = lo
            for ref, m in ((tab_a, a), (tab_at, a_t)):
                for w in (0, 1):
                    hi, lo = split(jnp.where(left64 if w == 0 else ~left64, m, 0.0))
                    ref[to, w, :64] = hi
                    ref[to, w, 64:] = lo
        return 0

    lax.fori_loop(0, count // 2, both, 0, unroll=2)


def prepare(src, experts, at, tables=()):
    vm = pl.BlockSpec(memory_space=pltpu.VMEM)
    return pl.pallas_call(
        functools.partial(prepare_kernel, at, src.shape[0] // 96),
        out_shape=[
            jax.ShapeDtypeStruct((experts, 2, 128, 128), BF16),
            jax.ShapeDtypeStruct((experts, 2, 128, 128), BF16),
            jax.ShapeDtypeStruct((experts, 64, 256), BF16),
            jax.ShapeDtypeStruct((experts, 64, 256), BF16),
            jax.ShapeDtypeStruct((experts, 64, 128), F32),
        ],
        in_specs=[vm] * (1 + len(tables)),
        out_specs=[vm] * 5,
        input_output_aliases={1 + i: i for i in range(len(tables))},
        compiler_params=pltpu.CompilerParams(vmem_limit_bytes=4 * MIB),
        cost_estimate=pl.CostEstimate(flops=1000, bytes_accessed=1000, transcendentals=0),
        name="prepare",
    )(src, *tables)


def pack_kernel(s, a, lam, out, held, sems):
    copies = [pltpu.make_async_copy(m, held.at[i], sems.at[i]) for i, m in enumerate((s, a, lam))]
    for copy in copies:
        copy.start()
    for i, copy in enumerate(copies):
        copy.wait()
        for p in range(s.shape[0] // 2):
            first = (3 * p + i) * 64
            out[first : first + 64, :] = jnp.concatenate([held[i, 2 * p], held[i, 2 * p + 1]], axis=1)


def pack_factors(*factors):
    slots = factors[0].shape[0]
    return pl.pallas_call(
        pack_kernel,
        out_shape=jax.ShapeDtypeStruct((slots * 96, 128), F32),
        in_specs=[pl.BlockSpec(memory_space=pltpu.HBM)] * 3,
        out_specs=pl.BlockSpec(memory_space=pltpu.VMEM),
        scratch_shapes=[pltpu.VMEM((3, slots, 64, 64), F32), pltpu.SemaphoreType.DMA((3,))],
        compiler_params=pltpu.CompilerParams(vmem_limit_bytes=4 * MIB),
        cost_estimate=pl.CostEstimate(flops=1000, bytes_accessed=1000, transcendentals=0),
        name="pack",
    )(*[pltpu.with_memory_space_constraint(m, pltpu.HBM) for m in factors])


def precondition_kernel(units, experts, size, queries, info, tab_a, tab_at, tab_s, tab_st, scale, *rest):
    chunks = len(units)
    raws, outs = rest[:chunks], rest[chunks : 2 * chunks]
    xs, ys = rest[2 * chunks :]
    left64 = lax.broadcasted_iota(jnp.int32, (64, 128), 1) < 64
    left = left64[:32]

    def pair(tab, e1, e2, three):
        hi = [tab[e1, 0, :64], tab[e2, 1, :64]]
        lo = [tab[e1, 0, 64:], tab[e2, 1, 64:]]
        return jnp.concatenate(hi + (hi if three else []) + lo, 0)

    def cross(tab, e1, e2, x):
        hi, lo = split(x)
        o = jnp.dot(
            jnp.concatenate([tab[e1], tab[e2]], 0),
            jnp.concatenate([hi, lo, hi, lo], 0),
            preferred_element_type=F32,
        )
        return jnp.where(left64, o[:64], o[64:])

    for ch in range(chunks):
        raw, out = raws[ch], outs[ch]
        first = size + experts + info[experts + units[ch]] * 8
        for c in range(32):
            xs[pl.ds(c * STRIDE, 64), :] = raw[:, c * 128 : (c + 1) * 128].astype(F32)

        def group(b, unused):
            es, g, x = [], [], []
            for i in range(GROUP):
                row = b * GROUP + i
                es.append(info[info[size + info[first + row % 8 * queries + row // 8]]])
                g.append(xs[pl.ds(row, 32, stride=STRIDE), :])
            n = GROUP // 2
            ee = [(es[2 * p], es[2 * p + 1]) for p in range(n)]
            for p in range(n):
                g1, g2 = g[2 * p], g[2 * p + 1]
                h = [jnp.where(left, g1, swap(g2)), jnp.where(left, swap(g1), g2)]
                h = jnp.concatenate(h, 0).astype(BF16)
                h = jnp.concatenate([h, h], 1)
                x.append(jnp.dot(h, pair(tab_a, *ee[p], False), preferred_element_type=F32))
            x = [
                cross(tab_st, *ee[p], x[p]) * jnp.where(left64, scale[ee[p][0]], scale[ee[p][1]])
                for p in range(n)
            ]
            x = [cross(tab_s, *ee[p], x[p]) for p in range(n)]
            for p in range(n):
                hi, lo = split(x[p])
                h = jnp.concatenate([hi, lo, hi], 1)
                y = jnp.dot(h, pair(tab_at, *ee[p], True), preferred_element_type=F32)
                top, low = y[:32], y[32:]
                for w, v in enumerate((jnp.where(left, top, swap(low)), jnp.where(left, swap(top), low))):
                    row = b * GROUP + 2 * p + w
                    ys[pl.ds((row % 8) * 8 + row // 8, 32, stride=STRIDE), :] = v
            return 0

        lax.fori_loop(0, 64 // GROUP, group, 0)
        for c in range(32):
            out[:, c * 128 : (c + 1) * 128] = ys[pl.ds(c * STRIDE, 64), :].astype(BF16)


def precondition(experts, size, queries, info, tables, raws, units):
    chunks = len(units)
    sm = pl.BlockSpec(memory_space=pltpu.SMEM)
    vm = pl.BlockSpec(memory_space=pltpu.VMEM)
    return pl.pallas_call(
        functools.partial(precondition_kernel, units, experts, size, queries),
        out_shape=[jax.ShapeDtypeStruct((64, raws[0].shape[1]), BF16)] * chunks,
        in_specs=[sm] + [vm] * (5 + len(raws)),
        out_specs=[vm] * chunks,
        scratch_shapes=[pltpu.VMEM((32 * STRIDE, 128), F32), pltpu.VMEM((32 * STRIDE, 128), F32)],
        compiler_params=pltpu.CompilerParams(vmem_limit_bytes=8 * MIB),
        cost_estimate=pl.CostEstimate(flops=1000, bytes_accessed=1000, transcendentals=0),
        name="precondition",
    )(info, *tables, *raws)


def products_kernel(units, placed, shapes, experts, info, route, query_route, train, *rest):
    n_in = len(shapes)
    n_old = 0 if placed is None else len(placed)
    parts, old = rest[:n_in], rest[n_in : n_in + n_old]
    out, held, total = rest[n_in + n_old :]
    blocks = sum(shapes) // 64
    train_rows = train.shape[0]
    at = 0
    for part, r in zip(parts, shapes):
        held[at : at + r, :] = part[...]
        at += r

    def tile(i, unused):
        here = pl.ds(pl.multiple_of(i * TILE, TILE), TILE)
        g = lax.dot_general(held[...], train[here, :], (((1,), (1,)), ((), ())), preferred_element_type=F32)
        there = route[:, here]
        for u in range(blocks):
            first = pl.multiple_of(info[experts + units[u]] * 64, 64)
            want = jnp.concatenate([query_route[pl.ds(first, 64), :]] * (TILE // 128), 1)
            hit = jnp.where(want == there, g[u * 64 : (u + 1) * 64], 0.0)
            total[u * 8 : (u + 1) * 8, here] = jnp.sum(hit.reshape(8, 8, TILE), axis=0)
        return 0

    lax.fori_loop(0, train_rows // TILE, tile, 0)
    row = lax.broadcasted_iota(jnp.int32, (train_rows, 128), 0)
    col = lax.broadcasted_iota(jnp.int32, (train_rows, 128), 1)
    fold = (lax.shift_right_logical(row, 3) == col).astype(BF16)
    x = total[...]
    hi = x.astype(BF16)
    left = x - hi.astype(F32)
    mid = left.astype(BF16)
    low = (left - mid.astype(F32)).astype(BF16)
    y = jnp.dot(jnp.concatenate([hi, mid, low], 0), fold, preferred_element_type=F32)
    n = blocks * 8
    y = y[:n] + y[n : 2 * n] + y[2 * n :]
    if placed is None:
        out[...] = y
        return
    todo = [(y, units)] + list(zip(old, placed))
    for values, names in todo:
        for u, name in enumerate(names):
            first = pl.multiple_of(info[experts + name] * 8, 8)
            out[pl.ds(first, 8), :] = values[u * 8 : (u + 1) * 8]


def products(info, experts, route, query_route, train, parts, units, old=None, placed=None, queries=0):
    shapes = [p.shape[0] for p in parts]
    blocks = sum(shapes) // 64
    train_rows, width = train.shape
    sm = pl.BlockSpec(memory_space=pltpu.SMEM)
    vm = pl.BlockSpec(memory_space=pltpu.VMEM)
    old = list(old or [])
    return pl.pallas_call(
        functools.partial(products_kernel, units, placed, shapes, experts),
        out_shape=jax.ShapeDtypeStruct((queries if placed else blocks * 8, 128), F32),
        in_specs=[sm] + [vm] * (3 + len(parts) + len(old)),
        out_specs=vm,
        scratch_shapes=[
            pltpu.VMEM((sum(shapes), width), BF16),
            pltpu.VMEM((blocks * 8, train_rows), F32),
        ],
        compiler_params=pltpu.CompilerParams(vmem_limit_bytes=14 * MIB),
        cost_estimate=pl.CostEstimate(flops=1000, bytes_accessed=1000, transcendentals=0),
        name="products",
    )(info, route, query_route, train, *parts, *old)


def tables_of(devices, slots):
    chips = devices // 2
    far = chips // 2
    ring = [2 * z for z in range(far)] + [2 * z + 1 for z in reversed(range(far))]
    spot = [ring.index(c) for c in range(chips)]
    rows = []
    for me in range(devices):
        place = []
        for slot in range(devices * slots):
            rel = (spot[slot // slots // 2] - spot[me // 2]) % chips
            order = chips - 1 if rel == far else 2 * (chips - rel) - 1 if rel > far else 2 * rel
            across = (slot // slots) % 2 != me % 2
            place.append((across * chips + order) * slots + slot % slots)
        near = []
        for d in range(far + 1):
            for core in (me % 2, 1 - me % 2):
                chip = ring[(spot[me // 2] + (d if core else -d)) % chips]
                near += [2 * chip + core, 2 * chip + 1 - core]
        rows.append(place + near)
    return ring, np.array(rows, np.int32)


def tie(value, other):
    return lax.optimization_barrier((value, other))[0]


def local(
    query_grads,
    query_routes,
    train_grads,
    train_routes,
    train_counts,
    owner_slot,
    basis_s,
    basis_a,
    eigenvalues,
):
    devices = lax.axis_size("shard")
    me = lax.axis_index("shard")
    experts = owner_slot.shape[0]
    queries, top = query_routes.shape
    width = query_grads.shape[2]
    train_dev = train_grads.shape[0]
    slots = basis_s.shape[0]
    chips = devices // 2
    far = chips // 2
    ring, constants = tables_of(devices, slots)
    info = lax.dynamic_index_in_dim(jnp.asarray(constants), me, 0, keepdims=False)
    size = info.shape[0]
    scalars = jnp.concatenate([info, owner_slot, query_routes.T.reshape(-1)])

    def shift(steps):
        return [
            (2 * c + k, 2 * ring[(i + steps[k]) % chips] + k) for i, c in enumerate(ring) for k in (0, 1)
        ]

    ahead, back, stream = shift((1, 1)), shift((-1, -1)), shift((1, -1))
    across = [(d, d ^ 1) for d in range(devices)]
    send = lambda v, way: lax.ppermute(v, "shard", way)

    raw = query_grads.reshape(-1, width)
    other_raw = send(raw, across)

    live = jnp.arange(train_dev, dtype=jnp.int32) < train_counts[0]
    route = jnp.where(live[:, None], train_routes, -1).reshape(1, train_dev * top)
    train = train_grads.reshape(train_dev * top, width)
    query_route = query_routes.reshape(devices, 8, top).transpose(0, 2, 1).reshape(queries * top, 1)
    query_route = jnp.broadcast_to(query_route, (queries * top, 128))

    pack = pack_factors(basis_s, basis_a, eigenvalues)
    cut = pack.shape[0] // 2
    ahead2, back2 = shift((2, 2)), shift((-2, -2))
    got, up, down, tables, crossed = [pack], pack, pack, (), 0
    for first in range(1, far, 2):
        if first == 3:
            up = tie(up, (other_raw, scalars, route, query_route))
        got += [send(up, ahead), send(down, back)]
        if first + 1 == far:
            got += [send(up[:cut], ahead2), send(down[cut:], back2)]
        else:
            up, down = send(up, ahead2), send(down, back2)
            got += [up, down]
        if first > 1 and first + 1 < far:
            continue
        mine = jnp.concatenate(got, axis=0)
        sib = send(mine, across)
        tables = prepare(mine, experts, crossed, tables)
        tables = prepare(sib, experts, experts // 2 + crossed, tables)
        crossed += mine.shape[0] // 96
        got = []
    near = send(tie(raw, up), stream)
    next_near = send(near, stream)

    pre = lambda *args: precondition(experts, size, queries, scalars, tables, *args)
    multiply = lambda parts, names, **more: products(
        scalars, experts, route, query_route, train, parts, names, **more
    )
    done, placed = [], []

    def work(units, after):
        parts = [v for p, _ in units for v in p]
        names = [n for _, ns in units for n in ns]
        parts[0] = tie(parts[0], after)
        done.append(multiply(parts, names))
        placed.append(names)
        return done[-1]

    both = lambda v, name: ([v, send(v, across)], [name, name + 2])
    (b,) = pre([tie(other_raw, near)], [1])
    own = ([send(b, across), b], [0, 1])
    b1 = send(b, stream)
    (a1,) = pre([tie(near, b)], [4])
    next_near = tie(next_near, a1)
    a3 = send(next_near, stream)
    (a2,) = pre([next_near], [8])
    b1 = tie(b1, a2)
    b2 = send(b1, stream)
    a3 = tie(a3, work([own, both(a1, 4)], b1))
    (a3,) = pre([a3], [12])
    a4 = send(a3, stream)
    b2 = tie(b2, work([both(a2, 8), both(b1, 5)], a3))
    b3 = send(b2, stream)
    b3 = tie(b3, work([both(a3, 12), both(b2, 9)], a4))
    coming, queue = [(a4, 16), (b3, 13)], []
    while len(coming) > 1:
        (now, name), (after, after_name) = coming
        last = 4 * far if name % 4 == 0 else 4 * far - 3
        further = [(send(now, stream), name + 4)] if name < last else []
        if queue:
            after = tie(after, work(queue, now))
        queue = [both(now, name)]
        coming = [(after, after_name)] + further
    units = queue + [both(*coming[0])]
    parts, names = [v for p, _ in units for v in p], [n for _, ns in units for n in ns]
    return multiply(parts, names, old=done, placed=placed, queries=queries)


def solution(mesh):
    placed = (
        P(("groups", "shard"), None, None),
        P("groups", None),
        P(("groups", "shard"), None, None),
        P(("groups", "shard"), None),
        P(("groups", "shard")),
        P(),
        P("shard", None, None),
        P("shard", None, None),
        P("shard", None, None),
    )
    return jax.shard_map(
        local, mesh=mesh, in_specs=placed, out_specs=P("groups", "shard"), check_vma=False
    )
```

```python
import functools

import jax
import jax.numpy as jnp
import numpy as np
from jax import lax
from jax.experimental import pallas as pl
from jax.experimental.pallas import tpu as pltpu
from jax.sharding import PartitionSpec as P

DAMPING = 0.01
F32, BF16 = jnp.float32, jnp.bfloat16
STRIDE = 65
GROUP = 64
TILE = 1024
MIB = 2**20


def split(x):
    hi = x.astype(BF16)
    return hi, (x - hi.astype(F32)).astype(BF16)


def swap(x):
    return pltpu.roll(x, 64, 1)


def prepare_kernel(at, count, src, *rest):
    tab_a, tab_at, tab_s, tab_st, scale = rest[-5:]
    left64 = lax.broadcasted_iota(jnp.int32, (64, 128), 1) < 64

    def both(pair, unused):
        e = 2 * pair
        base = pl.multiple_of(pair * 192, 192)
        f_s = jnp.concatenate([src[pl.ds(base + h, 32, stride=2), :] for h in (0, 1)], 0)
        f_a = src[pl.ds(base + 64, 64), :]
        f_l = src[pl.ds(base + 128, 64), :]

        def twice(f):
            r = swap(f)
            return jnp.where(left64, f, r), jnp.where(left64, r, f)

        for w0, (s, a, lam) in enumerate(zip(twice(f_s), twice(f_a), twice(f_l))):
            to = at + e + w0
            scale[to] = 1.0 / (lam + DAMPING)
            t = jnp.concatenate([s, a], 0).T[:64]
            r = swap(t)
            st, a_t = jnp.where(left64, t, r), jnp.where(left64, r, t)
            for ref, m in ((tab_s, s), (tab_st, st)):
                hi, lo = split(m)
                ref[to, :, :128] = hi
                ref[to, :, 128:] = lo
            for ref, m in ((tab_a, a), (tab_at, a_t)):
                for w in (0, 1):
                    hi, lo = split(jnp.where(left64 if w == 0 else ~left64, m, 0.0))
                    ref[to, w, :64] = hi
                    ref[to, w, 64:] = lo
        return 0

    lax.fori_loop(0, count // 2, both, 0, unroll=2)


def prepare(src, experts, at, tables=()):
    vm = pl.BlockSpec(memory_space=pltpu.VMEM)
    return pl.pallas_call(
        functools.partial(prepare_kernel, at, src.shape[0] // 96),
        out_shape=[
            jax.ShapeDtypeStruct((experts, 2, 128, 128), BF16),
            jax.ShapeDtypeStruct((experts, 2, 128, 128), BF16),
            jax.ShapeDtypeStruct((experts, 64, 256), BF16),
            jax.ShapeDtypeStruct((experts, 64, 256), BF16),
            jax.ShapeDtypeStruct((experts, 64, 128), F32),
        ],
        in_specs=[vm] * (1 + len(tables)),
        out_specs=[vm] * 5,
        input_output_aliases={1 + i: i for i in range(len(tables))},
        compiler_params=pltpu.CompilerParams(vmem_limit_bytes=4 * MIB),
        cost_estimate=pl.CostEstimate(flops=1000, bytes_accessed=1000, transcendentals=0),
        name="prepare",
    )(src, *tables)


def pack_kernel(s, a, lam, out, held, sems):
    copies = [pltpu.make_async_copy(m, held.at[i], sems.at[i]) for i, m in enumerate((s, a, lam))]
    for copy in copies:
        copy.start()
    for i, copy in enumerate(copies):
        copy.wait()
        for p in range(s.shape[0] // 2):
            first = (3 * p + i) * 64
            out[first : first + 64, :] = jnp.concatenate([held[i, 2 * p], held[i, 2 * p + 1]], axis=1)


def pack_factors(*factors):
    slots = factors[0].shape[0]
    return pl.pallas_call(
        pack_kernel,
        out_shape=jax.ShapeDtypeStruct((slots * 96, 128), F32),
        in_specs=[pl.BlockSpec(memory_space=pltpu.HBM)] * 3,
        out_specs=pl.BlockSpec(memory_space=pltpu.VMEM),
        scratch_shapes=[pltpu.VMEM((3, slots, 64, 64), F32), pltpu.SemaphoreType.DMA((3,))],
        compiler_params=pltpu.CompilerParams(vmem_limit_bytes=4 * MIB),
        cost_estimate=pl.CostEstimate(flops=1000, bytes_accessed=1000, transcendentals=0),
        name="pack",
    )(*[pltpu.with_memory_space_constraint(m, pltpu.HBM) for m in factors])


def precondition_kernel(units, experts, size, queries, info, tab_a, tab_at, tab_s, tab_st, scale, *rest):
    chunks = len(units)
    raws, outs = rest[:chunks], rest[chunks : 2 * chunks]
    xs, ys = rest[2 * chunks :]
    left64 = lax.broadcasted_iota(jnp.int32, (64, 128), 1) < 64
    left = left64[:32]

    def pair(tab, e1, e2, three):
        hi = [tab[e1, 0, :64], tab[e2, 1, :64]]
        lo = [tab[e1, 0, 64:], tab[e2, 1, 64:]]
        return jnp.concatenate(hi + (hi if three else []) + lo, 0)

    def cross(tab, e1, e2, x):
        hi, lo = split(x)
        o = jnp.dot(
            jnp.concatenate([tab[e1], tab[e2]], 0),
            jnp.concatenate([hi, lo, hi, lo], 0),
            preferred_element_type=F32,
        )
        return jnp.where(left64, o[:64], o[64:])

    for ch in range(chunks):
        raw, out = raws[ch], outs[ch]
        base = info[info.shape[0] - 1]
        first = size + experts + info[base + experts + units[ch]] * 8
        for c in range(32):
            xs[pl.ds(c * STRIDE, 64), :] = raw[:, c * 128 : (c + 1) * 128].astype(F32)

        def group(b, unused):
            es, g, x = [], [], []
            for i in range(GROUP):
                row = b * GROUP + i
                es.append(info[base + info[size + info[first + row % 8 * queries + row // 8]]])
                g.append(xs[pl.ds(row, 32, stride=STRIDE), :])
            n = GROUP // 2
            ee = [(es[2 * p], es[2 * p + 1]) for p in range(n)]
            for p in range(n):
                g1, g2 = g[2 * p], g[2 * p + 1]
                h = [jnp.where(left, g1, swap(g2)), jnp.where(left, swap(g1), g2)]
                h = jnp.concatenate(h, 0).astype(BF16)
                h = jnp.concatenate([h, h], 1)
                x.append(jnp.dot(h, pair(tab_a, *ee[p], False), preferred_element_type=F32))
            x = [
                cross(tab_st, *ee[p], x[p]) * jnp.where(left64, scale[ee[p][0]], scale[ee[p][1]])
                for p in range(n)
            ]
            x = [cross(tab_s, *ee[p], x[p]) for p in range(n)]
            for p in range(n):
                hi, lo = split(x[p])
                h = jnp.concatenate([hi, lo, hi], 1)
                y = jnp.dot(h, pair(tab_at, *ee[p], True), preferred_element_type=F32)
                top, low = y[:32], y[32:]
                for w, v in enumerate((jnp.where(left, top, swap(low)), jnp.where(left, swap(top), low))):
                    row = b * GROUP + 2 * p + w
                    ys[pl.ds((row % 8) * 8 + row // 8, 32, stride=STRIDE), :] = v
            return 0

        lax.fori_loop(0, 64 // GROUP, group, 0)
        for c in range(32):
            out[:, c * 128 : (c + 1) * 128] = ys[pl.ds(c * STRIDE, 64), :].astype(BF16)


def precondition(experts, size, queries, info, tables, raws, units):
    chunks = len(units)
    sm = pl.BlockSpec(memory_space=pltpu.SMEM)
    vm = pl.BlockSpec(memory_space=pltpu.VMEM)
    return pl.pallas_call(
        functools.partial(precondition_kernel, units, experts, size, queries),
        out_shape=[jax.ShapeDtypeStruct((64, raws[0].shape[1]), BF16)] * chunks,
        in_specs=[sm] + [vm] * (5 + len(raws)),
        out_specs=[vm] * chunks,
        scratch_shapes=[pltpu.VMEM((32 * STRIDE, 128), F32), pltpu.VMEM((32 * STRIDE, 128), F32)],
        compiler_params=pltpu.CompilerParams(vmem_limit_bytes=8 * MIB),
        cost_estimate=pl.CostEstimate(flops=1000, bytes_accessed=1000, transcendentals=0),
        name="precondition",
    )(info, *tables, *raws)


def products_kernel(units, placed, shapes, experts, info, route, query_route, train, *rest):
    n_in = len(shapes)
    n_old = 0 if placed is None else len(placed)
    parts, old = rest[:n_in], rest[n_in : n_in + n_old]
    out, held, total = rest[n_in + n_old :]
    blocks = sum(shapes) // 64
    train_rows = train.shape[0]
    base = info[info.shape[0] - 1]
    at = 0
    for part, r in zip(parts, shapes):
        held[at : at + r, :] = part[...]
        at += r

    def tile(i, unused):
        here = pl.ds(pl.multiple_of(i * TILE, TILE), TILE)
        g = lax.dot_general(held[...], train[here, :], (((1,), (1,)), ((), ())), preferred_element_type=F32)
        there = route[:, here]
        for u in range(blocks):
            first = pl.multiple_of(info[base + experts + units[u]] * 64, 64)
            want = jnp.concatenate([query_route[pl.ds(first, 64), :]] * (TILE // 128), 1)
            hit = jnp.where(want == there, g[u * 64 : (u + 1) * 64], 0.0)
            total[u * 8 : (u + 1) * 8, here] = jnp.sum(hit.reshape(8, 8, TILE), axis=0)
        return 0

    lax.fori_loop(0, train_rows // TILE, tile, 0)
    row = lax.broadcasted_iota(jnp.int32, (train_rows, 128), 0)
    col = lax.broadcasted_iota(jnp.int32, (train_rows, 128), 1)
    fold = (lax.shift_right_logical(row, 3) == col).astype(BF16)
    x = total[...]
    hi = x.astype(BF16)
    left = x - hi.astype(F32)
    mid = left.astype(BF16)
    low = (left - mid.astype(F32)).astype(BF16)
    y = jnp.dot(jnp.concatenate([hi, mid, low], 0), fold, preferred_element_type=F32)
    n = blocks * 8
    y = y[:n] + y[n : 2 * n] + y[2 * n :]
    if placed is None:
        out[...] = y
        return
    todo = [(y, units)] + list(zip(old, placed))
    for values, names in todo:
        for u, name in enumerate(names):
            first = pl.multiple_of(info[base + experts + name] * 8, 8)
            out[pl.ds(first, 8), :] = values[u * 8 : (u + 1) * 8]


def products(info, experts, route, query_route, train, parts, units, old=None, placed=None, queries=0):
    shapes = [p.shape[0] for p in parts]
    blocks = sum(shapes) // 64
    train_rows, width = train.shape
    sm = pl.BlockSpec(memory_space=pltpu.SMEM)
    vm = pl.BlockSpec(memory_space=pltpu.VMEM)
    old = list(old or [])
    return pl.pallas_call(
        functools.partial(products_kernel, units, placed, shapes, experts),
        out_shape=jax.ShapeDtypeStruct((queries if placed else blocks * 8, 128), F32),
        in_specs=[sm] + [vm] * (3 + len(parts) + len(old)),
        out_specs=vm,
        scratch_shapes=[
            pltpu.VMEM((sum(shapes), width), BF16),
            pltpu.VMEM((blocks * 8, train_rows), F32),
        ],
        compiler_params=pltpu.CompilerParams(vmem_limit_bytes=14 * MIB),
        cost_estimate=pl.CostEstimate(flops=1000, bytes_accessed=1000, transcendentals=0),
        name="products",
    )(info, route, query_route, train, *parts, *old)


def tables_of(devices, slots):
    chips = devices // 2
    far = chips // 2
    ring = [2 * z for z in range(far)] + [2 * z + 1 for z in reversed(range(far))]
    spot = [ring.index(c) for c in range(chips)]
    rows = []
    for me in range(devices):
        place = []
        for slot in range(devices * slots):
            rel = (spot[slot // slots // 2] - spot[me // 2]) % chips
            order = chips - 1 if rel == far else 2 * (chips - rel) - 1 if rel > far else 2 * rel
            across = (slot // slots) % 2 != me % 2
            place.append((across * chips + order) * slots + slot % slots)
        near = []
        for d in range(far + 1):
            for core in (me % 2, 1 - me % 2):
                chip = ring[(spot[me // 2] + (d if core else -d)) % chips]
                near += [2 * chip + core, 2 * chip + 1 - core]
        rows.append(place + near)
    return ring, np.array(rows, np.int32)


def tie(value, other):
    return lax.optimization_barrier((value, other))[0]


def local(
    query_grads,
    query_routes,
    train_grads,
    train_routes,
    train_counts,
    owner_slot,
    basis_s,
    basis_a,
    eigenvalues,
):
    devices = lax.axis_size("shard")
    me = lax.axis_index("shard")
    experts = owner_slot.shape[0]
    queries, top = query_routes.shape
    width = query_grads.shape[2]
    train_dev = train_grads.shape[0]
    slots = basis_s.shape[0]
    chips = devices // 2
    far = chips // 2
    ring, constants = tables_of(devices, slots)
    size = constants.size
    mine_at = (me * constants.shape[1]).astype(jnp.int32).reshape(1)
    scalars = jnp.concatenate([jnp.asarray(constants.reshape(-1)), owner_slot, query_routes.T.reshape(-1), mine_at])

    def shift(steps):
        return [
            (2 * c + k, 2 * ring[(i + steps[k]) % chips] + k) for i, c in enumerate(ring) for k in (0, 1)
        ]

    ahead, back, stream = shift((1, 1)), shift((-1, -1)), shift((1, -1))
    across = [(d, d ^ 1) for d in range(devices)]
    send = lambda v, way: lax.ppermute(v, "shard", way)

    raw = query_grads.reshape(-1, width)
    other_raw = send(raw, across)

    live = jnp.arange(train_dev, dtype=jnp.int32) < train_counts[0]
    route = jnp.where(live[:, None], train_routes, -1).reshape(1, train_dev * top)
    train = train_grads.reshape(train_dev * top, width)
    query_route = query_routes.reshape(devices, 8, top).transpose(0, 2, 1).reshape(queries * top, 1)
    query_route = jnp.broadcast_to(query_route, (queries * top, 128))

    pack = pack_factors(basis_s, basis_a, eigenvalues)
    cut = pack.shape[0] // 2
    ahead2, back2 = shift((2, 2)), shift((-2, -2))
    got, up, down, tables, crossed = [pack], pack, pack, (), 0
    for first in range(1, far, 2):
        if first == 3:
            up = tie(up, (other_raw, scalars, route, query_route))
        got += [send(up, ahead), send(down, back)]
        if first + 1 == far:
            got += [send(up[:cut], ahead2), send(down[cut:], back2)]
        else:
            up, down = send(up, ahead2), send(down, back2)
            got += [up, down]
        if first > 1 and first + 1 < far:
            continue
        mine = jnp.concatenate(got, axis=0)
        sib = send(mine, across)
        tables = prepare(mine, experts, crossed, tables)
        tables = prepare(sib, experts, experts // 2 + crossed, tables)
        crossed += mine.shape[0] // 96
        got = []
    near = send(tie(raw, up), stream)
    next_near = send(near, stream)

    pre = lambda *args: precondition(experts, size, queries, scalars, tables, *args)
    multiply = lambda parts, names, **more: products(
        scalars, experts, route, query_route, train, parts, names, **more
    )
    done, placed = [], []

    def work(units, after):
        parts = [v for p, _ in units for v in p]
        names = [n for _, ns in units for n in ns]
        parts[0] = tie(parts[0], after)
        done.append(multiply(parts, names))
        placed.append(names)
        return done[-1]

    both = lambda v, name: ([v, send(v, across)], [name, name + 2])
    (b,) = pre([tie(other_raw, near)], [1])
    own = ([send(b, across), b], [0, 1])
    b1 = send(b, stream)
    (a,) = pre([tie(near, b)], [4])
    raw_a, b, pending = tie(next_near, a), b1, [own, both(a, 4)]
    for step in range(2, far):
        next_a = send(raw_a, stream)
        (a,) = pre([raw_a], [4 * step])
        b = tie(b, a)
        next_b = send(b, stream)
        raw_a = tie(next_a, work(pending, b))
        pending = [both(a, 4 * step), both(b, 4 * step - 3)]
        b = next_b
    (a,) = pre([raw_a], [4 * far])
    b = tie(b, work(pending, a))
    units = [both(a, 4 * far), both(b, 4 * far - 3)]
    parts, names = [v for p, _ in units for v in p], [n for _, ns in units for n in ns]
    return multiply(parts, names, old=done, placed=placed, queries=queries)


def solution(mesh):
    placed = (
        P(("groups", "shard"), None, None),
        P("groups", None),
        P(("groups", "shard"), None, None),
        P(("groups", "shard"), None),
        P(("groups", "shard")),
        P(),
        P("shard", None, None),
        P("shard", None, None),
        P("shard", None, None),
    )
    return jax.shard_map(
        local, mesh=mesh, in_specs=placed, out_specs=P("groups", "shard"), check_vma=False
    )
```
